256 devices in a mesh: gx: 64 (over y, z, x_hi), gy: 4 (over x_lo, core).
Axes of the slice: x: 4 (x_hi: 2, x_lo: 2; x = x_hi * 2 + x_lo), y: 4, z: 8, core: 2. Of those that a mesh axis runs over, the one named last changes fastest.
Arguments:
- positions: float32 [3, 64, 4, 128], P(None, 'gx', 'gy'), may hold values from 0 to 1
- atom_features: float32 [64, 4, 128, 128], P('gx', 'gy'), may hold values from -6 to 6
- atom_count: int32 [64, 4], P('gx', 'gy'), may hold values from 80 to 128, as said below
- edge_count: int32 [64, 4], P('gx', 'gy'), may hold values from 192 to 512, as said below
- centers: int32 [64, 4, 512], P('gx', 'gy'), may hold values from 0 to 127, as said below
- neighbours: int32 [64, 4, 512], P('gx', 'gy'), may hold values from 0 to 303, as said below
- send_across: int32 [64, 4, 2, 64], P('gx', 'gy'), may hold values from 0 to 127, as said below
- send_along: int32 [64, 4, 2, 16], P('gx', 'gy'), may hold values from 0 to 127, as said below
- send_corner: int32 [64, 4, 4, 4], P('gx', 'gy'), may hold values from 0 to 127, as said below
- radial_weight: float32 [8, 128], replicated, may hold values from -2 to 2
- pair_weight: float32 [2, 128, 128], replicated, may hold values from -0.5 to 0.5
- tensor_weight: float32 [128, 64], replicated, may hold values from -0.5 to 0.5
- first_gate: float32 [128, 64], replicated, may hold values from -0.5 to 0.5
- mix_weight: float32 [3, 64, 64], replicated, may hold values from -0.75 to 0.75
- first_latent: float32 [320, 128], replicated, may hold values from -0.3125 to 0.3125
- second_gate: float32 [128, 64], replicated, may hold values from -0.5 to 0.5
- second_latent: float32 [320, 128], replicated, may hold values from -0.3125 to 0.3125
- readout_weight: float32 [128, 128], replicated, may hold values from -0.5 to 0.5
- readout_vector: float32 [128], replicated, may hold values from -0.5 to 0.5
- self_weight: float32 [128], replicated, may hold values from -0.5 to 0.5
Outputs:
- forces: float32 [3, 64, 4, 128], P(None, 'gx', 'gy')
- atom_energy: float32 [64, 4, 128], P('gx', 'gy')
The draws below stay inside these ranges and needn't reach their ends.
Inputs may be any that keep to these rules, and one draw needn't show every extreme that they name: `atom_count`: live atoms are the first slots of a domain; some domain is full. Edge slots from edge_count on are padding; some domain is full. A live edge's center is a live atom, and centers never fall along the live edges. `neighbours`: a live edge's neighbour is a live atom of the domain or a ghost slot. `send_across`: each list names distinct live atoms of the sending domain. `send_along`: each list names distinct live atoms of the sending domain. `send_corner`: each list names distinct live atoms of the sending domain.
All inputs are finite; a program needn't handle non-finite values.
Results may differ from the reference program's by a relative error of at most 0.00015.
Values sent between devices are 32-bit elements; how exact they have to be, the bound alone decides.
A program may use at most 64 MiB of HBM per device.

```python
import math
import jax
import jax.numpy as jnp
from jax import lax

ATOMS = 128
EDGES = 512
FACE_X = 64
FACE_Y = 16
CORNER = 4
GHOSTS = 176
TABLE = 304
CHANNELS = 64
LATENT = 128
FEATS = 128
BASIS = 8
DOM_X = 64
DOM_Y = 4


def domain_loads(key):
    count_key, full_key, short_key = jax.random.split(key, 3)
    domains = DOM_X * DOM_Y
    live_atoms = jax.random.randint(count_key, (domains,), ATOMS * 5 // 8, ATOMS + 1)
    fullest = jax.random.randint(full_key, (), 0, domains)
    chosen = jnp.arange(domains) == fullest
    live_atoms = jnp.where(chosen, ATOMS, live_atoms)
    shortfall = jax.random.randint(short_key, (domains,), 0, EDGES // 4 + 1)
    shortfall = jnp.where(chosen, 0, shortfall)
    live_edges = live_atoms * (EDGES // ATOMS) - shortfall
    return (live_atoms.reshape(DOM_X, DOM_Y).astype(jnp.int32), live_edges.reshape(DOM_X, DOM_Y).astype(jnp.int32))


def pick_atoms(key, live_atoms, list_count, list_size):
    scores = jax.random.randint(key, (DOM_X, DOM_Y, list_count, ATOMS), 0, 4096)
    slot_ids = jnp.arange(ATOMS, dtype=jnp.int32)
    dead = (slot_ids[None, None, None, :] >= live_atoms[:, :, None, None]).astype(jnp.int32)
    ranked = (dead * 4096 + scores) * ATOMS + slot_ids[None, None, None, :]
    order = jnp.argsort(ranked, axis=-1)
    return order[..., :list_size].astype(jnp.int32)


def draw_atom_count(key, part):
    live_atoms, live_edges = domain_loads(key)
    return live_atoms


def draw_edge_count(key, part):
    live_atoms, live_edges = domain_loads(key)
    return live_edges


def draw_centers(key, part):
    live_atoms, live_edges = domain_loads(key)
    key = jax.random.fold_in(key, 3)
    slot_ids = jnp.arange(EDGES, dtype=jnp.int32)[None, None, :]
    ordered = slot_ids * live_atoms[:, :, None] // live_edges[:, :, None]
    padded = jax.random.randint(key, (DOM_X, DOM_Y, EDGES), 0, live_atoms[:, :, None])
    return jnp.where(slot_ids < live_edges[:, :, None], ordered, padded).astype(jnp.int32)


def draw_neighbours(key, part):
    live_atoms, live_edges = domain_loads(key)
    key = jax.random.fold_in(key, 4)
    pick_key, local_key, ghost_key, pad_key = jax.random.split(key, 4)
    shape = (DOM_X, DOM_Y, EDGES)
    which = jax.random.randint(pick_key, shape, 0, 2)
    local_ids = jax.random.randint(local_key, shape, 0, live_atoms[:, :, None])
    ghost_ids = ATOMS + jax.random.randint(ghost_key, shape, 0, GHOSTS)
    padded = jax.random.randint(pad_key, shape, 0, TABLE)
    slot_ids = jnp.arange(EDGES, dtype=jnp.int32)[None, None, :]
    chosen = jnp.where(which == 0, local_ids, ghost_ids)
    return jnp.where(slot_ids < live_edges[:, :, None], chosen, padded).astype(jnp.int32)


def draw_send_across(key, part):
    live_atoms, live_edges = domain_loads(key)
    key = jax.random.fold_in(key, 5)
    return pick_atoms(key, live_atoms, 2, FACE_X)


def draw_send_along(key, part):
    live_atoms, live_edges = domain_loads(key)
    key = jax.random.fold_in(key, 6)
    return pick_atoms(key, live_atoms, 2, FACE_Y)


def draw_send_corner(key, part):
    live_atoms, live_edges = domain_loads(key)
    key = jax.random.fold_in(key, 7)
    return pick_atoms(key, live_atoms, 4, CORNER)


def block_scale(key, dims, cuts, least, top_value):
    def one(position, shards_of):
        draws = jax.random.uniform(jax.random.fold_in(jax.random.fold_in(key, 6), position), (shards_of,), jnp.float32, least / len(cuts), top_value / len(cuts))
        return jnp.repeat(jnp.exp(draws), dims[position] // shards_of).reshape((-1,) + (1,) * (len(dims) - position - 1))

    loudness = one(*cuts[0])
    for cut in cuts[1:]:
        loudness = loudness * one(*cut)
    return loudness


def centred(key, extent, spread, bound, cuts=(), kind=jnp.bfloat16):
    gain = block_scale(key, extent, cuts, -0.22, 0.18) if cuts else 1.0
    entries = jax.random.normal(key, extent, jnp.float32) * spread * gain
    return jnp.minimum(jnp.maximum(entries, -bound), bound).astype(kind)


def setup_inputs(seed: int = 0) -> dict:
    streams_of = jax.random.split(jax.random.key(seed), 21)
    return {
        "positions": jnp.clip(1.0 * jax.random.uniform(streams_of[0], (3, DOM_X, DOM_Y, ATOMS), jnp.float32) ** block_scale(streams_of[0], (3, DOM_X, DOM_Y, ATOMS), ((1, 64), (2, 4)), -0.2, 0.2), 0.0, 1.0),
        "atom_features": centred(streams_of[1], (DOM_X, DOM_Y, FEATS, ATOMS), 1.0, 6.0, ((0, 64), (1, 4)), jnp.float32),
        "atom_count": draw_atom_count(jax.random.fold_in(streams_of[20], 71), 0),
        "edge_count": draw_edge_count(jax.random.fold_in(streams_of[20], 71), 0),
        "centers": draw_centers(jax.random.fold_in(streams_of[20], 71), 0),
        "neighbours": draw_neighbours(jax.random.fold_in(streams_of[20], 71), 0),
        "send_across": draw_send_across(jax.random.fold_in(streams_of[20], 71), 0),
        "send_along": draw_send_along(jax.random.fold_in(streams_of[20], 71), 0),
        "send_corner": draw_send_corner(jax.random.fold_in(streams_of[20], 71), 0),
        "radial_weight": centred(streams_of[9], (BASIS, LATENT), BASIS ** -0.5, 2.0, (), jnp.float32),
        "pair_weight": centred(streams_of[10], (2, FEATS, LATENT), FEATS ** -0.5, 0.5, (), jnp.float32),
        "tensor_weight": centred(streams_of[11], (LATENT, CHANNELS), LATENT ** -0.5, 0.5, (), jnp.float32),
        "first_gate": centred(streams_of[12], (LATENT, CHANNELS), LATENT ** -0.5, 0.5, (), jnp.float32),
        "mix_weight": centred(streams_of[13], (3, CHANNELS, CHANNELS), CHANNELS ** -0.5, 0.75, (), jnp.float32),
        "first_latent": centred(streams_of[14], (LATENT + 3 * CHANNELS, LATENT), (LATENT + 3 * CHANNELS) ** -0.5, 0.3125, (), jnp.float32),
        "second_gate": centred(streams_of[15], (LATENT, CHANNELS), LATENT ** -0.5, 0.5, (), jnp.float32),
        "second_latent": centred(streams_of[16], (LATENT + 3 * CHANNELS, LATENT), (LATENT + 3 * CHANNELS) ** -0.5, 0.3125, (), jnp.float32),
        "readout_weight": centred(streams_of[17], (LATENT, LATENT), LATENT ** -0.5, 0.5, (), jnp.float32),
        "readout_vector": centred(streams_of[18], (LATENT,), LATENT ** -0.5, 0.5, (), jnp.float32),
        "self_weight": centred(streams_of[19], (FEATS,), FEATS ** -0.5, 0.5, (), jnp.float32),
    }


pool_scale = 0.5
exact = lax.Precision.HIGHEST

def harmonics(direction):
    unit_x, unit_y, unit_z = (direction[0], direction[1], direction[2])
    root_three = math.sqrt(3.0)
    square = unit_x * unit_x + unit_y * unit_y + unit_z * unit_z
    return jnp.stack([jnp.ones_like(unit_x), unit_x, unit_y, unit_z, root_three * unit_x * unit_y, root_three * unit_y * unit_z, 0.5 * (3.0 * unit_z * unit_z - square), root_three * unit_x * unit_z, 0.5 * root_three * (unit_x * unit_x - unit_y * unit_y)])

def project(weight, inputs):
    return lax.dot_general(weight, inputs, (((0,), (0,)), ((), ())), precision=exact, preferred_element_type=jnp.float32)

def pooled(values, centre_ids, atoms):
    empty = jnp.zeros(values.shape[:-1] + (atoms,), jnp.float32)
    return pool_scale * empty.at[..., centre_ids].add(values)

def scalars(tensor, other):
    return jnp.stack([tensor[0] * other[0], lax.optimization_barrier(jnp.sum(tensor[1:4] * other[1:4], axis=0)), lax.optimization_barrier(jnp.sum(tensor[4:] * other[4:], axis=0))])

def couple(tensor, other, mix_weight):
    product = tensor * other[0:1] + other * tensor[0:1]
    vector_one, vector_two = (tensor[1:4], other[1:4])
    cross_term = jnp.stack([vector_one[1] * vector_two[2] - vector_one[2] * vector_two[1], vector_one[2] * vector_two[0] - vector_one[0] * vector_two[2], vector_one[0] * vector_two[1] - vector_one[1] * vector_two[0]])
    members = [product[0:1], product[1:4] + cross_term, product[4:]]
    mixed_out = [jnp.einsum('mce,cd->mde', member, mix_weight[degree], precision=exact) for degree, member in enumerate(members)]
    return jnp.concatenate(mixed_out, axis=0)

def update(latent, tensor_scalars, weight):
    stacked = jnp.concatenate([latent, tensor_scalars.reshape(-1, latent.shape[1])], axis=0)
    return latent + jax.nn.silu(project(weight, stacked))

def section_one(pos_table, proj_centre, proj_table, centre_ids, neighbour_ids, live_edges, radial_weight, tensor_weight, first_gate):
    displacement = pos_table[:, neighbour_ids] - pos_table[:, centre_ids]
    length = jnp.sqrt(lax.optimization_barrier(jnp.sum(displacement * displacement, axis=0)) + 0.25)
    shape_terms = harmonics(displacement / length)
    envelope = live_edges / (1.0 + 0.25 * length * length)
    basis_count = radial_weight.shape[0]
    spacing = 2.5 / (basis_count - 1)
    centre_points = 0.5 + spacing * jnp.arange(basis_count, dtype=jnp.float32)
    radial_basis = jnp.exp(-jnp.square((length[None, :] - centre_points[:, None]) / spacing))
    latent = jax.nn.silu(project(radial_weight, radial_basis) + proj_centre[:, centre_ids] + proj_table[:, neighbour_ids])
    tensor_gain = project(tensor_weight, latent)
    gate_gain = project(first_gate, latent)
    tensor_zero = shape_terms[:, None, :] * tensor_gain[None]
    environment = pooled(shape_terms[:, None, :] * (gate_gain * envelope)[None], centre_ids, proj_centre.shape[1])
    return (environment, (latent, tensor_zero, shape_terms, envelope))

def section_two(latent, tensor_zero, shape_terms, envelope, env_table, centre_ids, neighbour_ids, mix_weight, first_latent, second_gate, second_latent, readout_weight, readout_vector, atoms):
    own_env = env_table[:, :, centre_ids]
    tensor_one = couple(tensor_zero, own_env, mix_weight)
    latent_one = update(latent, scalars(tensor_zero, own_env), first_latent)
    gate_gain = project(second_gate, latent_one)
    second_env = pooled(shape_terms[:, None, :] * (gate_gain * envelope)[None], centre_ids, atoms)
    joint_env = second_env[:, :, centre_ids] + env_table[:, :, neighbour_ids]
    latent_two = update(latent_one, scalars(tensor_one, joint_env), second_latent)
    hidden = jax.nn.silu(project(readout_weight, latent_two))
    return envelope * project(readout_vector[:, None], hidden)[0]

def slot_offsets(atoms, across, along, corner):

    def block(step_x, step_y, count):
        return jnp.stack([jnp.full((count,), step_x, jnp.float32), jnp.full((count,), step_y, jnp.float32), jnp.zeros((count,), jnp.float32)])
    return jnp.concatenate([block(0.0, 0.0, atoms), block(-1.0, 0.0, across), block(1.0, 0.0, across), block(0.0, -1.0, along), block(0.0, 1.0, along), block(-1.0, -1.0, corner), block(-1.0, 1.0, corner), block(1.0, -1.0, corner), block(1.0, 1.0, corner)], axis=1)

def ghost_tables(values, send_across, send_along, send_corner):

    def taken(lists):
        shaped = lists.reshape(lists.shape[:2] + (1,) * (values.ndim - 3) + lists.shape[2:])
        shaped = jnp.broadcast_to(shaped, values.shape[:-1] + lists.shape[2:])
        return jnp.take_along_axis(values, shaped, axis=-1)

    def rolled(block, step_x, step_y):
        return jnp.roll(block, (step_x, step_y), axis=(0, 1))
    pieces = [values, rolled(taken(send_across[:, :, 1]), 1, 0), rolled(taken(send_across[:, :, 0]), -1, 0), rolled(taken(send_along[:, :, 1]), 0, 1), rolled(taken(send_along[:, :, 0]), 0, -1), rolled(taken(send_corner[:, :, 3]), 1, 1), rolled(taken(send_corner[:, :, 2]), 1, -1), rolled(taken(send_corner[:, :, 1]), -1, 1), rolled(taken(send_corner[:, :, 0]), -1, -1)]
    return jnp.concatenate(pieces, axis=-1)

def map_domains(function, operands):
    domains = operands[0].shape[0]
    group_size = 8 if domains % 8 == 0 else 1
    shaped = tuple((member.reshape((domains // group_size, group_size) + member.shape[1:]) for member in operands))
    result = lax.map(jax.checkpoint(jax.vmap(lambda packed: function(*packed))), shaped)
    return result.reshape((domains,) + result.shape[2:])

def reference(positions, atom_features, atom_count, edge_count, centers, neighbours, send_across, send_along, send_corner, radial_weight, pair_weight, tensor_weight, first_gate, mix_weight, first_latent, second_gate, second_latent, readout_weight, readout_vector, self_weight):
    dom_x, dom_y = atom_count.shape
    domains = dom_x * dom_y
    atoms = positions.shape[3]
    edges = centers.shape[2]
    offsets = slot_offsets(atoms, send_across.shape[3], send_along.shape[3], send_corner.shape[3])
    slot_ids = jnp.arange(edges, dtype=jnp.int32)
    live_flat = (slot_ids[None, None, :] < edge_count[:, :, None]).astype(jnp.float32).reshape(domains, edges)
    feat_table = ghost_tables(atom_features, send_across, send_along, send_corner)
    table_size = feat_table.shape[-1]
    feat_flat = feat_table.reshape(domains, feat_table.shape[2], table_size)
    centre_flat = centers.reshape(domains, edges)
    neighbour_flat = neighbours.reshape(domains, edges)

    def first(pos_table, feats, centre_ids, neighbour_ids, live_edges):
        proj_centre = project(pair_weight[0], feats[:, :atoms])
        proj_table = project(pair_weight[1], feats)
        return section_one(pos_table, proj_centre, proj_table, centre_ids, neighbour_ids, live_edges, radial_weight, tensor_weight, first_gate)

    def second(pos_table, feats, centre_ids, neighbour_ids, live_edges, env_table):
        carried = first(pos_table, feats, centre_ids, neighbour_ids, live_edges)[1]
        return section_two(*carried, env_table, centre_ids, neighbour_ids, mix_weight, first_latent, second_gate, second_latent, readout_weight, readout_vector, atoms)

    def energy(pos_all):
        pos_table = ghost_tables(jnp.moveaxis(pos_all, 0, 2), send_across, send_along, send_corner) + offsets
        pos_flat = pos_table.reshape(domains, 3, table_size)
        environment = map_domains(lambda *packed: first(*packed)[0], (pos_flat, feat_flat, centre_flat, neighbour_flat, live_flat))
        channels = environment.shape[2]
        env_table = ghost_tables(environment.reshape(dom_x, dom_y, 9, channels, atoms), send_across, send_along, send_corner).reshape(domains, 9, channels, table_size)
        edge_energy = map_domains(second, (pos_flat, feat_flat, centre_flat, neighbour_flat, live_flat, env_table))
        return (jnp.sum(edge_energy), edge_energy)
    gradient, edge_energy = jax.grad(energy, has_aux=True)(positions)
    per_atom = jax.vmap(lambda values, ids: jnp.zeros((atoms,), jnp.float32).at[ids].add(values))(edge_energy, centre_flat).reshape(dom_x, dom_y, atoms)
    self_terms = jnp.einsum('xyfa,f->xya', atom_features, self_weight, precision=exact)
    alive = (jnp.arange(atoms, dtype=jnp.int32)[None, None, :] < atom_count[:, :, None]).astype(jnp.float32)
    return (-gradient, alive * (per_atom + self_terms))
```

```python
import functools
import math

import jax
import jax.numpy as jnp
from jax import lax
from jax.experimental import pallas as pl
from jax.experimental.pallas import tpu as pltpu
from jax.sharding import PartitionSpec as P

f32 = jnp.float32
bf16 = jnp.bfloat16

ATOMS = 128
EDGES = 512
CH = 64
LAT = 128
BASIS = 8
WIDTH = 2.5 / (BASIS - 1)
ROOT3 = math.sqrt(3.0)
DEGREE = (0, 1, 1, 1, 2, 2, 2, 2, 2)
STEPS = ((1, 0), (-1, 0), (0, 1), (0, -1), (1, 1), (1, -1), (-1, 1), (-1, -1))
FIRST_LANE = (0, 64, 0, 16, 32, 36, 40, 44)
LANES = (64, 64, 16, 16, 4, 4, 4, 4)
PACK_ONE = ((2, 72), (2, 72), (6, 24), (6, 24), (18, 8), (18, 8), (18, 8), (18, 8))
PACK_TWO = ((2, 288), (2, 288), (8, 72), (8, 72), (24, 24), (24, 24), (24, 24), (24, 24))


def split(value):
    high = value.astype(bf16)
    return high, (value - high.astype(f32)).astype(bf16)


def mm(left, right):
    return jnp.dot(left, right, preferred_element_type=f32)


def side_by_side(value):
    return jnp.concatenate(split(value), axis=1)


def stacked(value):
    return jnp.concatenate(split(value), axis=0)


def weight_form(weight):
    high, low = split(weight)
    top = jnp.concatenate([high, high], axis=1)
    bottom = jnp.concatenate([low, jnp.zeros_like(low)], axis=1)
    return jnp.concatenate([top, bottom], axis=0)


def dense(form, stack):
    both = mm(form, stack)
    rows = both.shape[0] // 2
    return both[:rows] + both[rows:]


def iota(shape, axis):
    return lax.broadcasted_iota(jnp.int32, shape, axis)


def hot(mask):
    return jnp.where(mask, 1.0, 0.0).astype(bf16)


def rolled(value, shift):
    shift = shift % 128
    return value if shift == 0 else pltpu.roll(value, shift, 1)


def sigmoid_parts(value):
    gate = 1.0 / (1.0 + jnp.exp(-value))
    act = value * gate
    return act, gate + act * (1.0 - gate)


def body(
    grid,
    pos_ref, feat_ref, atom_count_ref, edge_count_ref, centre_ref, neigh_ref,
    across_ref, along_ref, corner_ref, radial_ref, pair_ref, tensor_ref, gate1_ref,
    mix_ref, latent1_ref, gate2_ref, latent2_ref, readout_ref, vector_ref, self_ref,
    force_ref, energy_ref,
    *scratch,
):
    scratch = list(scratch)

    def take(count):
        taken = scratch[:count]
        del scratch[:count]
        return taken

    out1, in1, out2, in2, out3, in3, in4 = (take(8) for _ in range(7))
    out4 = take(2)
    (
        hcn, hcnt, sel, selt, table1, table2, geo, lat, grads, big,
        g1, t1, joint, wide, mixed, pile, acc, env_own,
        pair_t, first_form, first_back, gate2_form, gate2_back, mix_form, mix_back, latent1_form,
        latent1_back, latent2_form, latent2_back, readout_form, readout_back, vector_col,
        radial_form, radial_back, gate_pair,
    ) = take(35)
    send_sem, recv_sem = take(2)

    def drow(m):
        return m * 8

    size_x, size_y = grid
    ix, iy = lax.axis_index("gx"), lax.axis_index("gy")

    def device(step, sign):
        dx, dy = step
        return (
            lax.rem(ix + (sign * dx + size_x), size_x),
            lax.rem(iy + (sign * dy + size_y), size_y),
        )

    still = lax.div(ix, size_x)

    def lat_rows(first):
        return lat[pl.ds(pl.multiple_of(still * 8, 8) + first, 128)]

    barrier = pltpu.get_barrier_semaphore()
    for step in STEPS:
        pl.semaphore_signal(
            barrier, inc=1, device_id=device(step, 1), device_id_type=pl.DeviceIdType.MESH
        )

    def copy(phase, k, source, target, sign):
        return pltpu.make_async_remote_copy(
            src_ref=source,
            dst_ref=target,
            send_sem=send_sem.at[phase, k],
            recv_sem=recv_sem.at[phase, k],
            device_id=device(STEPS[k], sign),
            device_id_type=pl.DeviceIdType.MESH,
        )

    lane = iota((8, 128), 1)

    def pack(plan, k, table, target):
        groups, rows = plan[k]
        at = lane[:1]
        total = None
        for g in range(groups):
            piece = rolled(table[g * rows : (g + 1) * rows], LANES[k] * g - FIRST_LANE[k])
            total = piece if g == 0 else jnp.where(at >= LANES[k] * g, piece, total)
        target[...] = total

    def unpack_x(plan, ins):
        at = lane[:1]
        low, high = ins[0][...], ins[1][...]
        top = jnp.where(at < 64, low, rolled(high, 64))
        bottom = jnp.where(at < 64, rolled(low, 64), high)
        return jnp.concatenate([top, bottom], axis=0)

    def unpack_s(plan, ins):
        at = lane[:1]
        step = plan[4][1]
        pieces = []
        for b in range(plan[4][0]):
            value = None
            for k in range(2, 8):
                rows = plan[k][1]
                g, first = (b * step) // rows, (b * step) % rows
                piece = rolled(ins[k][first : first + step], FIRST_LANE[k] - LANES[k] * g)
                value = piece if k == 2 else jnp.where(at >= FIRST_LANE[k], piece, value)
            pieces.append(value)
        return jnp.concatenate(pieces, axis=0)

    across, along, corner = across_ref[0, 0], along_ref[0, 0], corner_ref[0, 0]
    list_x = jnp.concatenate([across[1:2], across[0:1]], axis=1)
    list_s = jnp.concatenate(
        [along[1:2], along[0:1], corner[3:4], corner[2:3], corner[1:2], corner[0:1],
         jnp.full((1, 80), -1, jnp.int32)],
        axis=1,
    )
    lists = jnp.concatenate([list_x, list_s], axis=1)
    chosen = hot(iota((128, 256), 0) == lists)
    sel[0:128] = chosen
    sel[128:256] = chosen

    sub8 = iota((8, 128), 0)
    features = feat_ref[0, 0]
    pos_own = jnp.where(
        sub8 == 0, pos_ref[0, 0],
        jnp.where(sub8 == 1, pos_ref[1, 0], jnp.where(sub8 == 2, pos_ref[2, 0], 0.0)),
    )
    pos_high = pos_own.astype(bf16).astype(f32)
    pos_mid = (pos_own - pos_high).astype(bf16).astype(f32)
    pos_low = pos_own - pos_high - pos_mid
    raw = side_by_side(jnp.concatenate([features, pos_own, pos_low], axis=0))
    sent = mm(raw, sel[...])
    sent = jnp.concatenate([sent[:128], sent[128:136] + sent[136:144], sent[136:144]], axis=0)
    for k in range(8):
        pack(PACK_ONE, k, sent[:, 0:128] if k < 2 else sent[:, 128:256], out1[k])

    pl.semaphore_wait(barrier, 8)
    first_copies = [copy(0, k, out1[k], in1[k], 1) for k in range(8)]
    for one in first_copies:
        one.start()

    centre_row, neigh_row = centre_ref[0], neigh_ref[0]
    hot_c = hot(iota((128, EDGES), 0) == centre_row)
    hot_n = [hot(iota((128, EDGES), 0) + 128 * t == neigh_row) for t in range(3)]
    for t, value in enumerate([hot_c] + hot_n):
        hcn[256 * t : 256 * t + 128] = value
        hcn[256 * t + 128 : 256 * t + 256] = value
    centre_col = jnp.transpose(jnp.broadcast_to(centre_row.astype(f32), (128, EDGES)))
    neigh_col = jnp.transpose(jnp.broadcast_to(neigh_row.astype(f32), (128, EDGES)))
    lane_f = iota((1, 128), 1).astype(f32)
    hot_ct = hot(centre_col == lane_f)
    hot_nt = [hot(neigh_col == lane_f + 128.0 * t) for t in range(3)]
    for t, value in enumerate([hot_ct] + hot_nt):
        hcnt[0:EDGES, 128 * t : 128 * t + 128] = value
        hcnt[EDGES : 2 * EDGES, 128 * t : 128 * t + 128] = value
    selt_f = jnp.transpose(chosen.astype(f32)).astype(bf16)
    for t in range(2):
        selt[256 * t : 256 * t + 128] = selt_f[128 * t : 128 * t + 128]
        selt[256 * t + 128 : 256 * t + 256] = selt_f[128 * t : 128 * t + 128]

    def forward_form(weight):
        return weight_form(jnp.transpose(weight))

    def pair_form(first):
        both = jnp.transpose(first)
        high, low = split(both)
        low = jnp.where(iota((1, 128), 1) < 64, low.astype(f32), 0.0).astype(bf16)
        return jnp.concatenate([high, low], axis=0)

    pair_t[...] = forward_form(pair_ref[1])
    own_raw = stacked(features)
    table1[:, 0:256] = side_by_side(dense(forward_form(pair_ref[0]), own_raw))
    table1[:, 256:512] = side_by_side(dense(pair_t[...], own_raw))
    self_rows = jnp.broadcast_to(self_ref[...].reshape(1, LAT), (16, LAT))
    self_row = dense(weight_form(self_rows), own_raw)[0:1]
    zeros64 = jnp.zeros((64, LAT), f32)
    first_t = jnp.concatenate([jnp.transpose(tensor_ref[...]), jnp.transpose(gate1_ref[...])], axis=0)
    first_form[...] = weight_form(first_t)
    first_back[...] = forward_form(first_t)
    gate2_t = jnp.transpose(gate2_ref[...])
    gate2_form[...] = weight_form(gate2_t)
    gate2_back[...] = forward_form(jnp.concatenate([gate2_t, zeros64], axis=0))
    for d in range(3):
        weight = mix_ref[d]
        turned = jnp.transpose(weight)
        mix_form[d] = pair_form(jnp.concatenate([weight, weight], axis=0))
        mix_back[d] = pair_form(jnp.concatenate([turned, turned], axis=0))
    latent1_form[...] = forward_form(jnp.concatenate([latent1_ref[...], zeros64], axis=0))
    latent1_back[...] = weight_form(latent1_ref[...])
    latent2_form[...] = forward_form(jnp.concatenate([latent2_ref[...], zeros64], axis=0))
    latent2_back[...] = weight_form(latent2_ref[...])
    readout_form[...] = forward_form(readout_ref[...])
    readout_back[...] = weight_form(readout_ref[...])
    vector_col[...] = jnp.transpose(jnp.broadcast_to(vector_ref[...].reshape(1, LAT), (128, LAT)))
    radial_full = jnp.concatenate([radial_ref[...], jnp.zeros((120, LAT), f32)], axis=0)
    radial_form[...] = forward_form(radial_full)
    radial_back[...] = weight_form(radial_full[:16])

    for one in first_copies:
        one.wait()
    table_x, table_s = unpack_x(PACK_ONE, in1), unpack_s(PACK_ONE, in1)
    ghost_raw = jnp.concatenate([table_x[:128], table_s[:128]], axis=1)
    ghost_proj = dense(pair_t[...], stacked(ghost_raw))
    table1[:, 512:768] = side_by_side(ghost_proj[:, 0:128])
    table1[:, 768:1024] = side_by_side(ghost_proj[:, 128:256])

    def offsets(rows):
        total = jnp.zeros((8, 128), f32)
        for k in rows:
            dx, dy = STEPS[k]
            inside = (lane >= FIRST_LANE[k]) & (lane < FIRST_LANE[k] + LANES[k])
            total = jnp.where(inside & (sub8 == 0), -1.0 * dx, total)
            total = jnp.where(inside & (sub8 == 1), -1.0 * dy, total)
        return total

    positions = jnp.concatenate(
        [pos_own, table_x[128:136] + offsets((0, 1)), table_s[128:136] + offsets(range(2, 8))], axis=1
    )
    p_high = positions.astype(bf16).astype(f32)
    p_mid = (positions - p_high).astype(bf16).astype(f32)
    p_low = positions - p_high - p_mid
    parts = jnp.concatenate([p_high, p_mid, p_low, jnp.zeros_like(p_low)], axis=0).astype(bf16)
    moved = mm(parts[:, 0:128], hcn[256:384] - hcn[0:128])
    moved += mm(parts[:, 128:256], hcn[512:640]) + mm(parts[:, 256:384], hcn[768:896])
    moved = moved[0:8] + moved[8:16] + moved[16:24]

    length = jnp.sqrt(jnp.sum(moved * moved, axis=0, keepdims=True) + 0.25)
    inverse = 1.0 / length
    unit = moved * inverse
    ux, uy, uz = unit[0:1], unit[1:2], unit[2:3]
    live = (iota((1, EDGES), 1) < edge_count_ref[0, 0]).astype(f32)
    falloff = 1.0 / (1.0 + 0.25 * length * length)
    envelope = live * falloff
    square = ux * ux + uy * uy + uz * uz
    shapes = [
        jnp.ones_like(ux), ux, uy, uz, ROOT3 * ux * uy, ROOT3 * uy * uz,
        0.5 * (3.0 * uz * uz - square), ROOT3 * ux * uz, 0.5 * ROOT3 * (ux * ux - uy * uy),
    ]
    for m in range(9):
        geo[drow(m) : drow(m) + 8] = jnp.broadcast_to(shapes[m], (8, EDGES))
    geo[72:80] = jnp.broadcast_to(envelope, (8, EDGES))

    mid_points = 0.5 + WIDTH * iota((BASIS, EDGES), 0).astype(f32)
    scaled = (length - mid_points) / WIDTH
    basis = jnp.exp(-(scaled * scaled))
    basis_full = jnp.concatenate([basis, jnp.zeros((120, EDGES), f32)], axis=0)
    before0 = dense(radial_form[...], stacked(basis_full)) + mm(table1[...], hcn[...])
    latent0, slope0 = sigmoid_parts(before0)
    lat[0:128] = slope0
    lat[128:256] = latent0
    high0, low0 = split(latent0)
    pile[0:128] = high0
    pile[384:512] = low0
    gains = dense(first_form[...], jnp.concatenate([high0, low0], axis=0))
    grads[0:128] = gains

    def lanes_at(t):
        return pl.ds(pl.multiple_of(t * 128, 128), 128)

    def shape_at(m, at):
        return geo[m * 8 : m * 8 + 1, at]

    def write_wide(row, t, value):
        high, low = split(value)
        wide[row : row + 16, lanes_at(t)] = high
        wide[row : row + 16, lanes_at(t + 4)] = low

    def spread(source, row0):
        def tile(t, carry):
            at = lanes_at(t)
            weight = 0.5 * geo[72:73, at]
            for c in range(4):
                gate = source[row0 + 16 * c : row0 + 16 * c + 16, at] * weight
                for m in range(9):
                    value = gate if m == 0 else gate * shape_at(m, at)
                    write_wide(64 * m + 16 * c, t, value)
            return carry

        lax.fori_loop(0, 4, tile, 0)

    spread(grads, 64)
    environment = mm(wide[...], hcnt[:, 0:128])
    env_pair = side_by_side(environment)
    table2[:, 256:512] = env_pair
    sent = mm(env_pair, sel[...])
    second_copies = [copy(1, k, out2[k], in2[k], 1) for k in range(8)]
    for k in range(8):
        pack(PACK_TWO, k, sent[:, 0:128] if k < 2 else sent[:, 128:256], out2[k])
        second_copies[k].start()

    g1[...] = mm(env_pair, hcn[0:256])

    def couple(t, carry):
        at = lanes_at(t)
        y = [None] + [shape_at(m, at) for m in range(1, 9)]
        for c in range(4):
            gain = grads[16 * c : 16 * c + 16, at]
            g = [g1[64 * m + 16 * c : 64 * m + 16 * c + 16, at] for m in range(9)]
            inner = [g[0] + g[0]] + [y[m] * g[0] + g[m] for m in range(1, 9)]
            inner[1] = inner[1] + (y[2] * g[3] - y[3] * g[2])
            inner[2] = inner[2] + (y[3] * g[1] - y[1] * g[3])
            inner[3] = inner[3] + (y[1] * g[2] - y[2] * g[1])
            for m in range(9):
                high, low = split(gain * inner[m])
                mixed[m, 16 * c : 16 * c + 16, at] = high
                mixed[m, 64 + 16 * c : 80 + 16 * c, at] = low
            sums = [
                g[0],
                y[1] * g[1] + y[2] * g[2] + y[3] * g[3],
                y[4] * g[4] + y[5] * g[5] + y[6] * g[6] + y[7] * g[7] + y[8] * g[8],
            ]
            for d in range(3):
                high, low = split(gain * sums[d])
                row = 128 + 64 * d + 16 * c
                pile[row : row + 16, at] = high
                pile[384 + row : 400 + row, at] = low
        return carry

    lax.fori_loop(0, 4, couple, 0)
    nothing = jnp.zeros((64, EDGES), bf16)
    pile[320:384] = nothing
    pile[704:768] = nothing
    act1, slope1 = sigmoid_parts(dense(latent1_form[...], pile[...]))
    lat[256:384] = slope1
    latent1 = lat_rows(128) + act1
    lat[384:512] = latent1
    high1, low1 = split(latent1)
    pile[0:128] = high1
    pile[384:512] = low1
    grads[128:192] = dense(gate2_form[...], jnp.concatenate([high1, low1], axis=0))
    spread(grads, 128)
    table2[:, 0:256] = side_by_side(mm(wide[...], hcnt[:, 0:128]))
    joint[...] = mm(table2[:, 0:512], hcn[0:512])
    for m in range(9):
        t1[64 * m : 64 * m + 64] = dense(mix_form[DEGREE[m]], mixed[m])

    for k in range(2):
        second_copies[k].wait()
    table2[:, 512:768] = side_by_side(unpack_x(PACK_TWO, in2))
    for k in range(2, 8):
        second_copies[k].wait()
    table2[:, 768:1024] = side_by_side(unpack_s(PACK_TWO, in2))
    joint[...] += mm(table2[:, 512:1024], hcn[512:1024])

    def contract(t, carry):
        at = lanes_at(t)
        for c in range(4):
            sums = [None, None, None]
            for m in range(9):
                row = 64 * m + 16 * c
                term = t1[row : row + 16, at] * joint[row : row + 16, at]
                d = DEGREE[m]
                sums[d] = term if sums[d] is None else sums[d] + term
            for d in range(3):
                high, low = split(sums[d])
                row = 128 + 64 * d + 16 * c
                pile[row : row + 16, at] = high
                pile[384 + row : 400 + row, at] = low
        return carry

    lax.fori_loop(0, 4, contract, 0)
    act2, slope2 = sigmoid_parts(dense(latent2_form[...], pile[...]))
    latent2 = lat_rows(384) + act2
    hidden, slope_h = sigmoid_parts(dense(readout_form[...], stacked(latent2)))
    vector_wide = jnp.concatenate([vector_col[...]] * 4, axis=1)
    energy_raw = jnp.sum(vector_wide * hidden, axis=0, keepdims=True)
    edge_energy = envelope * energy_raw

    d_hidden = vector_wide * envelope * slope_h
    d_latent2 = dense(readout_back[...], stacked(d_hidden))
    d_pile = dense(latent2_back[...], stacked(d_latent2 * slope2))
    lat[512:640] = d_latent2 + d_pile[0:128]
    grads[192:384] = d_pile[128:320]

    def joint_back(t, carry):
        at = lanes_at(t)
        for c in range(4):
            d_sum = [grads[192 + 64 * d + 16 * c : 208 + 64 * d + 16 * c, at] for d in range(3)]
            for m in range(9):
                row = 64 * m + 16 * c
                write_wide(row, t, t1[row : row + 16, at] * d_sum[DEGREE[m]])
        return carry

    lax.fori_loop(0, 4, joint_back, 0)
    back = mm(wide[...], hcnt[:, 256:512])
    third_copies = [copy(2, k, out3[k], in3[k], -1) for k in range(8)]
    for k in range(8):
        pack(PACK_TWO, k, back[:, 0:128] if k < 2 else back[:, 128:256], out3[k])
        third_copies[k].start()

    back = mm(wide[...], hcnt[:, 0:256])
    env_own[...] = back[:, 128:256]
    big[...] = mm(side_by_side(back[:, 0:128]), hcn[0:256])

    def mix_grads(t, carry):
        at = lanes_at(t)
        for c in range(4):
            d_sum = [grads[192 + 64 * d + 16 * c : 208 + 64 * d + 16 * c, at] for d in range(3)]
            for m in range(9):
                row = 64 * m + 16 * c
                high, low = split(joint[row : row + 16, at] * d_sum[DEGREE[m]])
                mixed[m, 16 * c : 16 * c + 16, at] = high
                mixed[m, 64 + 16 * c : 80 + 16 * c, at] = low
        return carry

    lax.fori_loop(0, 4, mix_grads, 0)
    for m in range(9):
        joint[64 * m : 64 * m + 64] = dense(mix_back[DEGREE[m]], mixed[m])

    def halves(value):
        return value[0:8] + value[8:16]

    def spread_back(source, row0, target0, fresh):
        def tile(t, carry):
            at = lanes_at(t)
            half = 0.5 * geo[72:73, at]
            d_shape = [None] * 9
            d_env = None
            for c in range(4):
                gate = source[row0 + 16 * c : row0 + 16 * c + 16, at]
                weight = gate * half
                total = None
                for m in range(9):
                    row = 64 * m + 16 * c
                    value = big[row : row + 16, at]
                    if m:
                        term = halves(value * weight)
                        d_shape[m] = term if c == 0 else d_shape[m] + term
                        value = value * shape_at(m, at)
                    total = value if m == 0 else total + value
                grads[target0 + 16 * c : target0 + 16 * c + 16, at] = total * half
                term = halves(total * gate)
                d_env = term if c == 0 else d_env + term
            d_env = 0.5 * d_env
            for m in range(1, 9):
                if fresh:
                    acc[drow(m) : drow(m) + 8, at] = d_shape[m]
                else:
                    acc[drow(m) : drow(m) + 8, at] += d_shape[m]
            if fresh:
                acc[0:8, at] = d_env
            else:
                acc[0:8, at] += d_env
            return carry

        lax.fori_loop(0, 4, tile, 0)

    spread_back(grads, 128, 384, True)
    gate_high, gate_low = split(grads[384:448])
    gate_pair[0:64] = gate_high
    gate_pair[64:128] = nothing
    gate_pair[128:192] = gate_low
    gate_pair[192:256] = nothing
    d_latent1 = lat_rows(512) + dense(gate2_back[...], gate_pair[...])
    d_pile = dense(latent1_back[...], stacked(d_latent1 * lat_rows(256)))
    lat[640:768] = d_latent1 + d_pile[0:128]
    grads[192:384] = d_pile[128:320]

    def couple_back(t, carry):
        at = lanes_at(t)
        y = [None] + [shape_at(m, at) for m in range(1, 9)]
        d_shape = [None] * 9
        for c in range(4):
            gain = grads[16 * c : 16 * c + 16, at]
            g = [g1[64 * m + 16 * c : 64 * m + 16 * c + 16, at] for m in range(9)]
            u = [joint[64 * m + 16 * c : 64 * m + 16 * c + 16, at] for m in range(9)]
            s = [grads[192 + 64 * d + 16 * c : 208 + 64 * d + 16 * c, at] for d in range(3)]
            inner = [g[0] + g[0]] + [y[m] * g[0] + g[m] for m in range(1, 9)]
            inner[1] = inner[1] + (y[2] * g[3] - y[3] * g[2])
            inner[2] = inner[2] + (y[3] * g[1] - y[1] * g[3])
            inner[3] = inner[3] + (y[1] * g[2] - y[2] * g[1])
            d_gain = s[0] * g[0]
            for m in range(9):
                d_gain = d_gain + u[m] * inner[m]
            d_gain = d_gain + s[1] * (y[1] * g[1] + y[2] * g[2] + y[3] * g[3])
            d_gain = d_gain + s[2] * (
                y[4] * g[4] + y[5] * g[5] + y[6] * g[6] + y[7] * g[7] + y[8] * g[8]
            )
            grads[448 + 16 * c : 464 + 16 * c, at] = d_gain
            k = [gain * value for value in u]
            q = [gain * value for value in s]
            d_g = [k[0] + k[0] + q[0]] + [k[m] + q[DEGREE[m]] * y[m] for m in range(1, 9)]
            for m in range(1, 9):
                d_g[0] = d_g[0] + k[m] * y[m]
            d_g[1] = d_g[1] + (k[2] * y[3] - k[3] * y[2])
            d_g[2] = d_g[2] + (k[3] * y[1] - k[1] * y[3])
            d_g[3] = d_g[3] + (k[1] * y[2] - k[2] * y[1])
            d_y = [None] + [k[m] * g[0] + q[DEGREE[m]] * g[m] for m in range(1, 9)]
            d_y[1] = d_y[1] + (k[3] * g[2] - k[2] * g[3])
            d_y[2] = d_y[2] + (k[1] * g[3] - k[3] * g[1])
            d_y[3] = d_y[3] + (k[2] * g[1] - k[1] * g[2])
            for m in range(1, 9):
                term = halves(d_y[m])
                d_shape[m] = term if c == 0 else d_shape[m] + term
            for m in range(9):
                write_wide(64 * m + 16 * c, t, d_g[m])
        for m in range(1, 9):
            acc[drow(m) : drow(m) + 8, at] += d_shape[m]
        return carry

    lax.fori_loop(0, 4, couple_back, 0)
    env_own[...] += mm(wide[...], hcnt[:, 0:128])

    for one in third_copies:
        one.wait()
    ghosts = jnp.concatenate(
        [side_by_side(unpack_x(PACK_TWO, in3)), side_by_side(unpack_s(PACK_TWO, in3))], axis=1
    )
    d_environment = env_own[...] + mm(ghosts, selt[...])
    big[...] = mm(side_by_side(d_environment), hcn[0:256])
    spread_back(grads, 64, 512, False)
    d_latent0 = lat_rows(640) + dense(first_back[...], stacked(grads[448:576]))
    d_basis = dense(radial_back[...], stacked(d_latent0 * lat_rows(0)))[:8]
    d_length = jnp.sum(d_basis * basis * scaled, axis=0, keepdims=True) * (-2.0 / WIDTH)
    d_env = jnp.sum(acc[0:8], axis=0, keepdims=True) + energy_raw
    d_length = d_length - 0.5 * length * envelope * falloff * d_env
    d_y = [None] + [jnp.sum(acc[drow(m) : drow(m) + 8], axis=0, keepdims=True) for m in range(1, 9)]
    d_ux = d_y[1] + ROOT3 * (uy * d_y[4] + uz * d_y[7] + ux * d_y[8]) - ux * d_y[6]
    d_uy = d_y[2] + ROOT3 * (ux * d_y[4] + uz * d_y[5] - uy * d_y[8]) - uy * d_y[6]
    d_uz = d_y[3] + ROOT3 * (uy * d_y[5] + ux * d_y[7]) + 2.0 * (uz * d_y[6])
    d_length = d_length - (d_ux * ux + d_uy * uy + d_uz * uz) * inverse
    sub_e = iota((8, EDGES), 0)
    d_unit = jnp.where(sub_e == 0, d_ux, jnp.where(sub_e == 1, d_uy, jnp.where(sub_e == 2, d_uz, 0.0)))
    d_moved = d_unit * inverse + d_length * unit

    def folded(value):
        high = value.astype(bf16).astype(f32)
        return jnp.concatenate([high, value - high], axis=0).astype(bf16)

    d_parts = folded(d_moved)
    d_table = halves(mm(d_parts, hcnt[0:EDGES, 128:512]))
    d_centre = halves(mm(d_parts, hcnt[0:EDGES, 0:128]))
    out4[0][...] = d_table[:, 128:256]
    out4[1][...] = d_table[:, 256:384]
    last_copies = [copy(3, k, out4[0] if k < 2 else out4[1], in4[k], -1) for k in range(8)]
    for one in last_copies:
        one.start()
    d_own = d_table[:, 0:128] - d_centre

    per_atom = halves(mm(folded(jnp.broadcast_to(edge_energy, (8, EDGES))), hcnt[0:EDGES, 0:128]))[0:1]
    alive = (iota((1, ATOMS), 1) < atom_count_ref[0, 0]).astype(f32)
    energy_ref[0] = alive * (per_atom + self_row)

    for one in last_copies:
        one.wait()
    grad_x = jnp.where(lane < 64, in4[0][...], in4[1][...])
    grad_s = in4[2][...]
    for k in range(3, 8):
        grad_s = jnp.where(lane >= FIRST_LANE[k], in4[k][...], grad_s)
    returned = mm(folded(grad_x), selt[0:128]) + mm(folded(grad_s), selt[256:384])
    total = d_own + halves(returned)
    for axis in range(3):
        force_ref[axis, 0] = -total[axis : axis + 1]


def per_device(grid, *args):
    vmem = pl.BlockSpec(memory_space=pltpu.VMEM)
    smem = pl.BlockSpec(memory_space=pltpu.SMEM)
    specs = [vmem] * len(args)
    specs[2] = specs[3] = smem
    packs = [
        [pltpu.VMEM((plan[k][1], 128), f32) for k in range(8)] for plan in (PACK_ONE, PACK_TWO)
    ]
    small = [pltpu.VMEM((8, 128), f32)]
    scratch = packs[0] * 2 + packs[1] * 4 + small * 8 + small * 2
    scratch += [
        pltpu.VMEM((1024, EDGES), bf16),
        pltpu.VMEM((2 * EDGES, 512), bf16),
        pltpu.VMEM((256, 256), bf16),
        pltpu.VMEM((512, 128), bf16),
        pltpu.VMEM((128, 1024), bf16),
        pltpu.VMEM((576, 1024), bf16),
        pltpu.VMEM((80, EDGES), f32),
        pltpu.VMEM((768, EDGES), f32),
        pltpu.VMEM((576, EDGES), f32),
        pltpu.VMEM((576, EDGES), f32),
        pltpu.VMEM((576, EDGES), f32),
        pltpu.VMEM((576, EDGES), f32),
        pltpu.VMEM((576, EDGES), f32),
        pltpu.VMEM((576, 2 * EDGES), bf16),
        pltpu.VMEM((9, 128, EDGES), bf16),
        pltpu.VMEM((768, EDGES), bf16),
        pltpu.VMEM((72, EDGES), f32),
        pltpu.VMEM((576, 128), f32),
        *(
            pltpu.VMEM(shape, bf16)
            for shape in (
                (256, 256), (256, 256), (256, 256), (128, 256), (256, 256), (3, 128, 128),
                (3, 128, 128), (256, 768), (640, 256), (256, 768), (640, 256), (256, 256), (256, 256),
            )
        ),
        pltpu.VMEM((128, 128), f32),
        pltpu.VMEM((256, 256), bf16),
        pltpu.VMEM((32, 256), bf16),
        pltpu.VMEM((256, EDGES), bf16),
        pltpu.SemaphoreType.DMA((4, 8)),
        pltpu.SemaphoreType.DMA((4, 8)),
    ]
    return pl.pallas_call(
        functools.partial(body, grid),
        out_shape=(
            jax.ShapeDtypeStruct((3, 1, 1, ATOMS), f32),
            jax.ShapeDtypeStruct((1, 1, ATOMS), f32),
        ),
        in_specs=specs,
        out_specs=(vmem, vmem),
        scratch_shapes=scratch,
        compiler_params=pltpu.CompilerParams(
            collective_id=0, has_side_effects=True, vmem_limit_bytes=48 * 1024 * 1024
        ),
    )(*args)


def solution(mesh):
    grid = (mesh.shape["gx"], mesh.shape["gy"])
    edge = P("gx", "gy", None)
    lists = P("gx", "gy", None, None)
    return jax.shard_map(
        functools.partial(per_device, grid),
        mesh=mesh,
        in_specs=(P(None, "gx", "gy", None), lists, P("gx", "gy"), P("gx", "gy"), edge, edge)
        + (lists,) * 3
        + (P(),) * 11,
        out_specs=(P(None, "gx", "gy", None), edge),
        check_vma=False,
    )
```

```python
import functools
import math

import jax
import jax.numpy as jnp
from jax import lax
from jax.experimental import pallas as pl
from jax.experimental.pallas import tpu as pltpu
from jax.sharding import PartitionSpec as P

f32 = jnp.float32
bf16 = jnp.bfloat16

ATOMS = 128
EDGES = 512
CH = 64
LAT = 128
BASIS = 8
WIDTH = 2.5 / (BASIS - 1)
ROOT3 = math.sqrt(3.0)
DEGREE = (0, 1, 1, 1, 2, 2, 2, 2, 2)
STEPS = ((1, 0), (-1, 0), (0, 1), (0, -1), (1, 1), (1, -1), (-1, 1), (-1, -1))
FIRST_LANE = (0, 64, 0, 16, 32, 36, 40, 44)
LANES = (64, 64, 16, 16, 4, 4, 4, 4)
PACK_ONE = ((2, 72), (2, 72), (6, 24), (6, 24), (18, 8), (18, 8), (18, 8), (18, 8))
PACK_TWO = ((2, 288), (2, 288), (8, 72), (8, 72), (24, 24), (24, 24), (24, 24), (24, 24))


FETCH_FIRST = (0, 1, 4, 5, 6)


def split(value):
    high = value.astype(bf16)
    return high, (value - high.astype(f32)).astype(bf16)


def mm(left, right):
    return jnp.dot(left, right, preferred_element_type=f32)


def side_by_side(value):
    return jnp.concatenate(split(value), axis=1)


def stacked(value):
    return jnp.concatenate(split(value), axis=0)


def weight_form(weight):
    high, low = split(weight)
    top = jnp.concatenate([high, high], axis=1)
    bottom = jnp.concatenate([low, jnp.zeros_like(low)], axis=1)
    return jnp.concatenate([top, bottom], axis=0)


def dense(form, stack):
    both = mm(form, stack)
    rows = both.shape[0] // 2
    return both[:rows] + both[rows:]


def iota(shape, axis):
    return lax.broadcasted_iota(jnp.int32, shape, axis)


def hot(mask):
    return jnp.where(mask, 1.0, 0.0).astype(bf16)


def rolled(value, shift):
    shift = shift % 128
    return value if shift == 0 else pltpu.roll(value, shift, 1)


def sigmoid_parts(value):
    gate = 1.0 / (1.0 + jnp.exp(-value))
    act = value * gate
    return act, gate + act * (1.0 - gate)


def body(
    grid,
    atom_count_ref, edge_count_ref, *refs,
):
    sources, (force_ref, energy_ref), scratch = refs[:18], refs[18:20], refs[20:]
    scratch = list(scratch)

    (
        pos_ref, feat_ref, centre_ref, neigh_ref, across_ref, along_ref, corner_ref, radial_ref,
        pair_ref, tensor_ref, gate1_ref, mix_ref, latent1_ref, gate2_ref, latent2_ref, readout_ref,
        vector_ref, self_ref, fetch_sem,
    ) = scratch[:19]
    fetches = [
        pltpu.make_async_copy(source, target, fetch_sem.at[i])
        for i, (source, target) in enumerate(zip(sources, scratch[:18]))
    ]
    for i in FETCH_FIRST:
        fetches[i].start()
    for i in range(18):
        if i not in FETCH_FIRST:
            fetches[i].start()
    del scratch[:19]

    def take(count):
        taken = scratch[:count]
        del scratch[:count]
        return taken

    out1, in1, out2, in2, out3, in3, in4 = (take(8) for _ in range(7))
    out4 = take(2)
    (
        hcn, hcnt, sel, selt, table1, table2, geo, lat, grads, big,
        g1, t1, joint, wide, mixed, pile, acc, env_own,
        pair_t, first_form, first_back, gate2_form, gate2_back, mix_form, mix_back, latent1_form,
        latent1_back, latent2_form, latent2_back, readout_form, readout_back, vector_col,
        radial_form, radial_back, gate_pair,
    ) = take(35)
    send_sem, recv_sem = take(2)

    def drow(m):
        return m * 8

    size_x, size_y = grid
    ix, iy = lax.axis_index("gx"), lax.axis_index("gy")

    def device(step, sign):
        dx, dy = step
        return (
            lax.rem(ix + (sign * dx + size_x), size_x),
            lax.rem(iy + (sign * dy + size_y), size_y),
        )

    still = lax.div(ix, size_x)

    def lat_rows(first):
        return lat[pl.ds(pl.multiple_of(still * 8, 8) + first, 128)]

    barrier = pltpu.get_barrier_semaphore()
    for step in STEPS:
        pl.semaphore_signal(
            barrier, inc=1, device_id=device(step, 1), device_id_type=pl.DeviceIdType.MESH
        )

    def copy(phase, k, source, target, sign):
        return pltpu.make_async_remote_copy(
            src_ref=source,
            dst_ref=target,
            send_sem=send_sem.at[phase, k],
            recv_sem=recv_sem.at[phase, k],
            device_id=device(STEPS[k], sign),
            device_id_type=pl.DeviceIdType.MESH,
        )

    lane = iota((8, 128), 1)

    def pack(plan, k, table, target):
        groups, rows = plan[k]
        at = lane[:1]
        total = None
        for g in range(groups):
            piece = rolled(table[g * rows : (g + 1) * rows], LANES[k] * g - FIRST_LANE[k])
            total = piece if g == 0 else jnp.where(at >= LANES[k] * g, piece, total)
        target[...] = total

    def unpack_x(plan, ins):
        at = lane[:1]
        low, high = ins[0][...], ins[1][...]
        top = jnp.where(at < 64, low, rolled(high, 64))
        bottom = jnp.where(at < 64, rolled(low, 64), high)
        return jnp.concatenate([top, bottom], axis=0)

    def unpack_s(plan, ins):
        at = lane[:1]
        step = plan[4][1]
        pieces = []
        for b in range(plan[4][0]):
            value = None
            for k in range(2, 8):
                rows = plan[k][1]
                g, first = (b * step) // rows, (b * step) % rows
                piece = rolled(ins[k][first : first + step], FIRST_LANE[k] - LANES[k] * g)
                value = piece if k == 2 else jnp.where(at >= FIRST_LANE[k], piece, value)
            pieces.append(value)
        return jnp.concatenate(pieces, axis=0)

    for i in FETCH_FIRST:
        fetches[i].wait()

    across, along, corner = across_ref[0, 0], along_ref[0, 0], corner_ref[0, 0]
    list_x = jnp.concatenate([across[1:2], across[0:1]], axis=1)
    list_s = jnp.concatenate(
        [along[1:2], along[0:1], corner[3:4], corner[2:3], corner[1:2], corner[0:1],
         jnp.full((1, 80), -1, jnp.int32)],
        axis=1,
    )
    lists = jnp.concatenate([list_x, list_s], axis=1)
    chosen = hot(iota((128, 256), 0) == lists)
    sel[0:128] = chosen
    sel[128:256] = chosen

    sub8 = iota((8, 128), 0)
    features = feat_ref[0, 0]
    pos_own = jnp.where(
        sub8 == 0, pos_ref[0, 0],
        jnp.where(sub8 == 1, pos_ref[1, 0], jnp.where(sub8 == 2, pos_ref[2, 0], 0.0)),
    )
    pos_high = pos_own.astype(bf16).astype(f32)
    pos_mid = (pos_own - pos_high).astype(bf16).astype(f32)
    pos_low = pos_own - pos_high - pos_mid
    raw = side_by_side(jnp.concatenate([features, pos_own, pos_low], axis=0))
    sent = mm(raw, sel[...])
    sent = jnp.concatenate([sent[:128], sent[128:136] + sent[136:144], sent[136:144]], axis=0)
    for k in range(8):
        pack(PACK_ONE, k, sent[:, 0:128] if k < 2 else sent[:, 128:256], out1[k])

    pl.semaphore_wait(barrier, 8)
    first_copies = [copy(0, k, out1[k], in1[k], 1) for k in range(8)]
    for one in first_copies:
        one.start()

    for i in (2, 3):
        fetches[i].wait()
    centre_row, neigh_row = centre_ref[0], neigh_ref[0]
    hot_c = hot(iota((128, EDGES), 0) == centre_row)
    hot_n = [hot(iota((128, EDGES), 0) + 128 * t == neigh_row) for t in range(3)]
    for t, value in enumerate([hot_c] + hot_n):
        hcn[256 * t : 256 * t + 128] = value
        hcn[256 * t + 128 : 256 * t + 256] = value
    centre_col = jnp.transpose(jnp.broadcast_to(centre_row.astype(f32), (128, EDGES)))
    neigh_col = jnp.transpose(jnp.broadcast_to(neigh_row.astype(f32), (128, EDGES)))
    lane_f = iota((1, 128), 1).astype(f32)
    hot_ct = hot(centre_col == lane_f)
    hot_nt = [hot(neigh_col == lane_f + 128.0 * t) for t in range(3)]
    for t, value in enumerate([hot_ct] + hot_nt):
        hcnt[0:EDGES, 128 * t : 128 * t + 128] = value
        hcnt[EDGES : 2 * EDGES, 128 * t : 128 * t + 128] = value
    selt_f = jnp.transpose(chosen.astype(f32)).astype(bf16)
    for t in range(2):
        selt[256 * t : 256 * t + 128] = selt_f[128 * t : 128 * t + 128]
        selt[256 * t + 128 : 256 * t + 256] = selt_f[128 * t : 128 * t + 128]

    def forward_form(weight):
        return weight_form(jnp.transpose(weight))

    def pair_form(first):
        both = jnp.transpose(first)
        high, low = split(both)
        low = jnp.where(iota((1, 128), 1) < 64, low.astype(f32), 0.0).astype(bf16)
        return jnp.concatenate([high, low], axis=0)

    for i in range(7, 18):
        fetches[i].wait()
    pair_t[...] = forward_form(pair_ref[1])
    own_raw = stacked(features)
    table1[:, 0:256] = side_by_side(dense(forward_form(pair_ref[0]), own_raw))
    table1[:, 256:512] = side_by_side(dense(pair_t[...], own_raw))
    self_rows = jnp.broadcast_to(self_ref[...].reshape(1, LAT), (16, LAT))
    self_row = dense(weight_form(self_rows), own_raw)[0:1]
    zeros64 = jnp.zeros((64, LAT), f32)
    first_t = jnp.concatenate([tensor_ref[...], gate1_ref[...]], axis=0)
    first_form[...] = weight_form(first_t)
    first_back[...] = forward_form(first_t)
    gate2_t = gate2_ref[...]
    gate2_form[...] = weight_form(gate2_t)
    gate2_back[...] = forward_form(jnp.concatenate([gate2_t, zeros64], axis=0))
    for d in range(3):
        weight = mix_ref[d]
        turned = jnp.transpose(weight)
        mix_form[d] = pair_form(jnp.concatenate([weight, weight], axis=0))
        mix_back[d] = pair_form(jnp.concatenate([turned, turned], axis=0))
    latent1_form[...] = forward_form(jnp.concatenate([latent1_ref[...], zeros64], axis=0))
    latent1_back[...] = weight_form(latent1_ref[...])
    latent2_form[...] = forward_form(jnp.concatenate([latent2_ref[...], zeros64], axis=0))
    latent2_back[...] = weight_form(latent2_ref[...])
    readout_form[...] = forward_form(readout_ref[...])
    readout_back[...] = weight_form(readout_ref[...])
    vector_col[...] = jnp.transpose(jnp.broadcast_to(vector_ref[...].reshape(1, LAT), (128, LAT)))
    radial_full = jnp.concatenate([radial_ref[...], jnp.zeros((120, LAT), f32)], axis=0)
    radial_form[...] = forward_form(radial_full)
    radial_back[...] = weight_form(radial_full[:16])

    for one in first_copies:
        one.wait()
    table_x, table_s = unpack_x(PACK_ONE, in1), unpack_s(PACK_ONE, in1)
    ghost_raw = jnp.concatenate([table_x[:128], table_s[:128]], axis=1)
    ghost_proj = dense(pair_t[...], stacked(ghost_raw))
    table1[:, 512:768] = side_by_side(ghost_proj[:, 0:128])
    table1[:, 768:1024] = side_by_side(ghost_proj[:, 128:256])

    def offsets(rows):
        total = jnp.zeros((8, 128), f32)
        for k in rows:
            dx, dy = STEPS[k]
            inside = (lane >= FIRST_LANE[k]) & (lane < FIRST_LANE[k] + LANES[k])
            total = jnp.where(inside & (sub8 == 0), -1.0 * dx, total)
            total = jnp.where(inside & (sub8 == 1), -1.0 * dy, total)
        return total

    positions = jnp.concatenate(
        [pos_own, table_x[128:136] + offsets((0, 1)), table_s[128:136] + offsets(range(2, 8))], axis=1
    )
    p_high = positions.astype(bf16).astype(f32)
    p_mid = (positions - p_high).astype(bf16).astype(f32)
    p_low = positions - p_high - p_mid
    parts = jnp.concatenate([p_high, p_mid, p_low, jnp.zeros_like(p_low)], axis=0).astype(bf16)
    moved = mm(parts[:, 0:128], hcn[256:384] - hcn[0:128])
    moved += mm(parts[:, 128:256], hcn[512:640]) + mm(parts[:, 256:384], hcn[768:896])
    moved = moved[0:8] + moved[8:16] + moved[16:24]

    length = jnp.sqrt(jnp.sum(moved * moved, axis=0, keepdims=True) + 0.25)
    inverse = 1.0 / length
    unit = moved * inverse
    ux, uy, uz = unit[0:1], unit[1:2], unit[2:3]
    live = (iota((1, EDGES), 1) < edge_count_ref[0, 0]).astype(f32)
    falloff = 1.0 / (1.0 + 0.25 * length * length)
    envelope = live * falloff
    square = ux * ux + uy * uy + uz * uz
    shapes = [
        jnp.ones_like(ux), ux, uy, uz, ROOT3 * ux * uy, ROOT3 * uy * uz,
        0.5 * (3.0 * uz * uz - square), ROOT3 * ux * uz, 0.5 * ROOT3 * (ux * ux - uy * uy),
    ]
    for m in range(9):
        geo[drow(m) : drow(m) + 8] = jnp.broadcast_to(shapes[m], (8, EDGES))
    geo[72:80] = jnp.broadcast_to(envelope, (8, EDGES))

    mid_points = 0.5 + WIDTH * iota((BASIS, EDGES), 0).astype(f32)
    scaled = (length - mid_points) / WIDTH
    basis = jnp.exp(-(scaled * scaled))
    basis_full = jnp.concatenate([basis, jnp.zeros((120, EDGES), f32)], axis=0)
    before0 = dense(radial_form[...], stacked(basis_full)) + mm(table1[...], hcn[...])
    latent0, slope0 = sigmoid_parts(before0)
    lat[0:128] = slope0
    lat[128:256] = latent0
    high0, low0 = split(latent0)
    pile[0:128] = high0
    pile[384:512] = low0
    gains = dense(first_form[...], jnp.concatenate([high0, low0], axis=0))
    grads[0:128] = gains

    def lanes_at(t):
        return pl.ds(pl.multiple_of(t * 128, 128), 128)

    def shape_at(m, at):
        return geo[m * 8 : m * 8 + 1, at]

    def write_wide(row, t, value):
        high, low = split(value)
        wide[row : row + 16, lanes_at(t)] = high
        wide[row : row + 16, lanes_at(t + 4)] = low

    def spread(source, row0):
        def tile(t, carry):
            at = lanes_at(t)
            weight = 0.5 * geo[72:73, at]
            for c in range(4):
                gate = source[row0 + 16 * c : row0 + 16 * c + 16, at] * weight
                for m in range(9):
                    value = gate if m == 0 else gate * shape_at(m, at)
                    write_wide(64 * m + 16 * c, t, value)
            return carry

        lax.fori_loop(0, 4, tile, 0)

    spread(grads, 64)
    environment = mm(wide[...], hcnt[:, 0:128])
    env_pair = side_by_side(environment)
    table2[:, 256:512] = env_pair
    sent = mm(env_pair, sel[...])
    second_copies = [copy(1, k, out2[k], in2[k], 1) for k in range(8)]
    for k in range(8):
        pack(PACK_TWO, k, sent[:, 0:128] if k < 2 else sent[:, 128:256], out2[k])
        second_copies[k].start()

    g1[...] = mm(env_pair, hcn[0:256])

    def couple(t, carry):
        at = lanes_at(t)
        y = [None] + [shape_at(m, at) for m in range(1, 9)]
        for c in range(4):
            gain = grads[16 * c : 16 * c + 16, at]
            g = [g1[64 * m + 16 * c : 64 * m + 16 * c + 16, at] for m in range(9)]
            inner = [g[0] + g[0]] + [y[m] * g[0] + g[m] for m in range(1, 9)]
            inner[1] = inner[1] + (y[2] * g[3] - y[3] * g[2])
            inner[2] = inner[2] + (y[3] * g[1] - y[1] * g[3])
            inner[3] = inner[3] + (y[1] * g[2] - y[2] * g[1])
            for m in range(9):
                high, low = split(gain * inner[m])
                mixed[m, 16 * c : 16 * c + 16, at] = high
                mixed[m, 64 + 16 * c : 80 + 16 * c, at] = low
            sums = [
                g[0],
                y[1] * g[1] + y[2] * g[2] + y[3] * g[3],
                y[4] * g[4] + y[5] * g[5] + y[6] * g[6] + y[7] * g[7] + y[8] * g[8],
            ]
            for d in range(3):
                high, low = split(gain * sums[d])
                row = 128 + 64 * d + 16 * c
                pile[row : row + 16, at] = high
                pile[384 + row : 400 + row, at] = low
        return carry

    lax.fori_loop(0, 4, couple, 0)
    nothing = jnp.zeros((64, EDGES), bf16)
    pile[320:384] = nothing
    pile[704:768] = nothing
    act1, slope1 = sigmoid_parts(dense(latent1_form[...], pile[...]))
    lat[256:384] = slope1
    latent1 = lat_rows(128) + act1
    lat[384:512] = latent1
    high1, low1 = split(latent1)
    pile[0:128] = high1
    pile[384:512] = low1
    grads[128:192] = dense(gate2_form[...], jnp.concatenate([high1, low1], axis=0))
    spread(grads, 128)
    table2[:, 0:256] = side_by_side(mm(wide[...], hcnt[:, 0:128]))
    joint[...] = mm(table2[:, 0:512], hcn[0:512])
    for m in range(9):
        t1[64 * m : 64 * m + 64] = dense(mix_form[DEGREE[m]], mixed[m])

    for k in range(2):
        second_copies[k].wait()
    table2[:, 512:768] = side_by_side(unpack_x(PACK_TWO, in2))
    for k in range(2, 8):
        second_copies[k].wait()
    table2[:, 768:1024] = side_by_side(unpack_s(PACK_TWO, in2))
    joint[...] += mm(table2[:, 512:1024], hcn[512:1024])

    def contract(t, carry):
        at = lanes_at(t)
        for c in range(4):
            sums = [None, None, None]
            for m in range(9):
                row = 64 * m + 16 * c
                term = t1[row : row + 16, at] * joint[row : row + 16, at]
                d = DEGREE[m]
                sums[d] = term if sums[d] is None else sums[d] + term
            for d in range(3):
                high, low = split(sums[d])
                row = 128 + 64 * d + 16 * c
                pile[row : row + 16, at] = high
                pile[384 + row : 400 + row, at] = low
        return carry

    lax.fori_loop(0, 4, contract, 0)
    act2, slope2 = sigmoid_parts(dense(latent2_form[...], pile[...]))
    latent2 = lat_rows(384) + act2
    hidden, slope_h = sigmoid_parts(dense(readout_form[...], stacked(latent2)))
    vector_wide = jnp.concatenate([vector_col[...]] * 4, axis=1)
    energy_raw = jnp.sum(vector_wide * hidden, axis=0, keepdims=True)
    edge_energy = envelope * energy_raw

    d_hidden = vector_wide * envelope * slope_h
    d_latent2 = dense(readout_back[...], stacked(d_hidden))
    d_pile = dense(latent2_back[...], stacked(d_latent2 * slope2))
    lat[512:640] = d_latent2 + d_pile[0:128]
    grads[192:384] = d_pile[128:320]

    def joint_back(t, carry):
        at = lanes_at(t)
        for c in range(4):
            d_sum = [grads[192 + 64 * d + 16 * c : 208 + 64 * d + 16 * c, at] for d in range(3)]
            for m in range(9):
                row = 64 * m + 16 * c
                write_wide(row, t, t1[row : row + 16, at] * d_sum[DEGREE[m]])
        return carry

    lax.fori_loop(0, 4, joint_back, 0)
    back = mm(wide[...], hcnt[:, 256:512])
    third_copies = [copy(2, k, out3[k], in3[k], -1) for k in range(8)]
    for k in range(8):
        pack(PACK_TWO, k, back[:, 0:128] if k < 2 else back[:, 128:256], out3[k])
        third_copies[k].start()

    back = mm(wide[...], hcnt[:, 0:256])
    env_own[...] = back[:, 128:256]
    big[...] = mm(side_by_side(back[:, 0:128]), hcn[0:256])

    def mix_grads(t, carry):
        at = lanes_at(t)
        for c in range(4):
            d_sum = [grads[192 + 64 * d + 16 * c : 208 + 64 * d + 16 * c, at] for d in range(3)]
            for m in range(9):
                row = 64 * m + 16 * c
                high, low = split(joint[row : row + 16, at] * d_sum[DEGREE[m]])
                mixed[m, 16 * c : 16 * c + 16, at] = high
                mixed[m, 64 + 16 * c : 80 + 16 * c, at] = low
        return carry

    lax.fori_loop(0, 4, mix_grads, 0)
    for m in range(9):
        joint[64 * m : 64 * m + 64] = dense(mix_back[DEGREE[m]], mixed[m])

    def halves(value):
        return value[0:8] + value[8:16]

    def spread_back(source, row0, target0, fresh):
        def tile(t, carry):
            at = lanes_at(t)
            half = 0.5 * geo[72:73, at]
            d_shape = [None] * 9
            d_env = None
            for c in range(4):
                gate = source[row0 + 16 * c : row0 + 16 * c + 16, at]
                weight = gate * half
                total = None
                for m in range(9):
                    row = 64 * m + 16 * c
                    value = big[row : row + 16, at]
                    if m:
                        term = halves(value * weight)
                        d_shape[m] = term if c == 0 else d_shape[m] + term
                        value = value * shape_at(m, at)
                    total = value if m == 0 else total + value
                grads[target0 + 16 * c : target0 + 16 * c + 16, at] = total * half
                term = halves(total * gate)
                d_env = term if c == 0 else d_env + term
            d_env = 0.5 * d_env
            for m in range(1, 9):
                if fresh:
                    acc[drow(m) : drow(m) + 8, at] = d_shape[m]
                else:
                    acc[drow(m) : drow(m) + 8, at] += d_shape[m]
            if fresh:
                acc[0:8, at] = d_env
            else:
                acc[0:8, at] += d_env
            return carry

        lax.fori_loop(0, 4, tile, 0)

    spread_back(grads, 128, 384, True)
    gate_high, gate_low = split(grads[384:448])
    gate_pair[0:64] = gate_high
    gate_pair[64:128] = nothing
    gate_pair[128:192] = gate_low
    gate_pair[192:256] = nothing
    d_latent1 = lat_rows(512) + dense(gate2_back[...], gate_pair[...])
    d_pile = dense(latent1_back[...], stacked(d_latent1 * lat_rows(256)))
    lat[640:768] = d_latent1 + d_pile[0:128]
    grads[192:384] = d_pile[128:320]

    def couple_back(t, carry):
        at = lanes_at(t)
        y = [None] + [shape_at(m, at) for m in range(1, 9)]
        d_shape = [None] * 9
        for c in range(4):
            gain = grads[16 * c : 16 * c + 16, at]
            g = [g1[64 * m + 16 * c : 64 * m + 16 * c + 16, at] for m in range(9)]
            u = [joint[64 * m + 16 * c : 64 * m + 16 * c + 16, at] for m in range(9)]
            s = [grads[192 + 64 * d + 16 * c : 208 + 64 * d + 16 * c, at] for d in range(3)]
            inner = [g[0] + g[0]] + [y[m] * g[0] + g[m] for m in range(1, 9)]
            inner[1] = inner[1] + (y[2] * g[3] - y[3] * g[2])
            inner[2] = inner[2] + (y[3] * g[1] - y[1] * g[3])
            inner[3] = inner[3] + (y[1] * g[2] - y[2] * g[1])
            d_gain = s[0] * g[0]
            for m in range(9):
                d_gain = d_gain + u[m] * inner[m]
            d_gain = d_gain + s[1] * (y[1] * g[1] + y[2] * g[2] + y[3] * g[3])
            d_gain = d_gain + s[2] * (
                y[4] * g[4] + y[5] * g[5] + y[6] * g[6] + y[7] * g[7] + y[8] * g[8]
            )
            grads[448 + 16 * c : 464 + 16 * c, at] = d_gain
            k = [gain * value for value in u]
            q = [gain * value for value in s]
            d_g = [k[0] + k[0] + q[0]] + [k[m] + q[DEGREE[m]] * y[m] for m in range(1, 9)]
            for m in range(1, 9):
                d_g[0] = d_g[0] + k[m] * y[m]
            d_g[1] = d_g[1] + (k[2] * y[3] - k[3] * y[2])
            d_g[2] = d_g[2] + (k[3] * y[1] - k[1] * y[3])
            d_g[3] = d_g[3] + (k[1] * y[2] - k[2] * y[1])
            d_y = [None] + [k[m] * g[0] + q[DEGREE[m]] * g[m] for m in range(1, 9)]
            d_y[1] = d_y[1] + (k[3] * g[2] - k[2] * g[3])
            d_y[2] = d_y[2] + (k[1] * g[3] - k[3] * g[1])
            d_y[3] = d_y[3] + (k[2] * g[1] - k[1] * g[2])
            for m in range(1, 9):
                term = halves(d_y[m])
                d_shape[m] = term if c == 0 else d_shape[m] + term
            for m in range(9):
                write_wide(64 * m + 16 * c, t, d_g[m])
        for m in range(1, 9):
            acc[drow(m) : drow(m) + 8, at] += d_shape[m]
        return carry

    lax.fori_loop(0, 4, couple_back, 0)
    env_own[...] += mm(wide[...], hcnt[:, 0:128])

    for one in third_copies:
        one.wait()
    ghosts = jnp.concatenate(
        [side_by_side(unpack_x(PACK_TWO, in3)), side_by_side(unpack_s(PACK_TWO, in3))], axis=1
    )
    d_environment = env_own[...] + mm(ghosts, selt[...])
    big[...] = mm(side_by_side(d_environment), hcn[0:256])
    spread_back(grads, 64, 512, False)
    d_latent0 = lat_rows(640) + dense(first_back[...], stacked(grads[448:576]))
    d_basis = dense(radial_back[...], stacked(d_latent0 * lat_rows(0)))[:8]
    d_length = jnp.sum(d_basis * basis * scaled, axis=0, keepdims=True) * (-2.0 / WIDTH)
    d_env = jnp.sum(acc[0:8], axis=0, keepdims=True) + energy_raw
    d_length = d_length - 0.5 * length * envelope * falloff * d_env
    d_y = [None] + [jnp.sum(acc[drow(m) : drow(m) + 8], axis=0, keepdims=True) for m in range(1, 9)]
    d_ux = d_y[1] + ROOT3 * (uy * d_y[4] + uz * d_y[7] + ux * d_y[8]) - ux * d_y[6]
    d_uy = d_y[2] + ROOT3 * (ux * d_y[4] + uz * d_y[5] - uy * d_y[8]) - uy * d_y[6]
    d_uz = d_y[3] + ROOT3 * (uy * d_y[5] + ux * d_y[7]) + 2.0 * (uz * d_y[6])
    d_length = d_length - (d_ux * ux + d_uy * uy + d_uz * uz) * inverse
    sub_e = iota((8, EDGES), 0)
    d_unit = jnp.where(sub_e == 0, d_ux, jnp.where(sub_e == 1, d_uy, jnp.where(sub_e == 2, d_uz, 0.0)))
    d_moved = d_unit * inverse + d_length * unit

    def folded(value):
        high = value.astype(bf16).astype(f32)
        return jnp.concatenate([high, value - high], axis=0).astype(bf16)

    d_parts = folded(d_moved)
    d_table = halves(mm(d_parts, hcnt[0:EDGES, 128:512]))
    d_centre = halves(mm(d_parts, hcnt[0:EDGES, 0:128]))
    out4[0][...] = d_table[:, 128:256]
    out4[1][...] = d_table[:, 256:384]
    last_copies = [copy(3, k, out4[0] if k < 2 else out4[1], in4[k], -1) for k in range(8)]
    for one in last_copies:
        one.start()
    d_own = d_table[:, 0:128] - d_centre

    per_atom = halves(mm(folded(jnp.broadcast_to(edge_energy, (8, EDGES))), hcnt[0:EDGES, 0:128]))[0:1]
    alive = (iota((1, ATOMS), 1) < atom_count_ref[0, 0]).astype(f32)
    energy_ref[0] = alive * (per_atom + self_row)

    for one in last_copies:
        one.wait()
    grad_x = jnp.where(lane < 64, in4[0][...], in4[1][...])
    grad_s = in4[2][...]
    for k in range(3, 8):
        grad_s = jnp.where(lane >= FIRST_LANE[k], in4[k][...], grad_s)
    returned = mm(folded(grad_x), selt[0:128]) + mm(folded(grad_s), selt[256:384])
    total = d_own + halves(returned)
    for axis in range(3):
        force_ref[axis, 0] = -total[axis : axis + 1]


def per_device(grid, *args):
    args = list(args)
    for i in (11, 12, 15):
        args[i] = args[i].T
    counts, sources = args[2:4], args[:2] + args[4:]
    vmem = pl.BlockSpec(memory_space=pltpu.VMEM)
    smem = pl.BlockSpec(memory_space=pltpu.SMEM)
    specs = [smem] * 2 + [pl.BlockSpec(memory_space=pltpu.HBM)] * 18
    packs = [
        [pltpu.VMEM((plan[k][1], 128), f32) for k in range(8)] for plan in (PACK_ONE, PACK_TWO)
    ]
    small = [pltpu.VMEM((8, 128), f32)]
    scratch = [pltpu.VMEM(source.shape, source.dtype) for source in sources]
    scratch += [pltpu.SemaphoreType.DMA((18,))]
    scratch += packs[0] * 2 + packs[1] * 4 + small * 8 + small * 2
    scratch += [
        pltpu.VMEM((1024, EDGES), bf16),
        pltpu.VMEM((2 * EDGES, 512), bf16),
        pltpu.VMEM((256, 256), bf16),
        pltpu.VMEM((512, 128), bf16),
        pltpu.VMEM((128, 1024), bf16),
        pltpu.VMEM((576, 1024), bf16),
        pltpu.VMEM((80, EDGES), f32),
        pltpu.VMEM((768, EDGES), f32),
        pltpu.VMEM((576, EDGES), f32),
        pltpu.VMEM((576, EDGES), f32),
        pltpu.VMEM((576, EDGES), f32),
        pltpu.VMEM((576, EDGES), f32),
        pltpu.VMEM((576, EDGES), f32),
        pltpu.VMEM((576, 2 * EDGES), bf16),
        pltpu.VMEM((9, 128, EDGES), bf16),
        pltpu.VMEM((768, EDGES), bf16),
        pltpu.VMEM((72, EDGES), f32),
        pltpu.VMEM((576, 128), f32),
        *(
            pltpu.VMEM(shape, bf16)
            for shape in (
                (256, 256), (256, 256), (256, 256), (128, 256), (256, 256), (3, 128, 128),
                (3, 128, 128), (256, 768), (640, 256), (256, 768), (640, 256), (256, 256), (256, 256),
            )
        ),
        pltpu.VMEM((128, 128), f32),
        pltpu.VMEM((256, 256), bf16),
        pltpu.VMEM((32, 256), bf16),
        pltpu.VMEM((256, EDGES), bf16),
        pltpu.SemaphoreType.DMA((4, 8)),
        pltpu.SemaphoreType.DMA((4, 8)),
    ]
    return pl.pallas_call(
        functools.partial(body, grid),
        out_shape=(
            jax.ShapeDtypeStruct((3, 1, 1, ATOMS), f32),
            jax.ShapeDtypeStruct((1, 1, ATOMS), f32),
        ),
        in_specs=specs,
        out_specs=(vmem, vmem),
        scratch_shapes=scratch,
        compiler_params=pltpu.CompilerParams(
            collective_id=0, has_side_effects=True, vmem_limit_bytes=64 * 1024 * 1024
        ),
    )(*counts, *sources)


def solution(mesh):
    grid = (mesh.shape["gx"], mesh.shape["gy"])
    edge = P("gx", "gy", None)
    lists = P("gx", "gy", None, None)
    return jax.shard_map(
        functools.partial(per_device, grid),
        mesh=mesh,
        in_specs=(P(None, "gx", "gy", None), lists, P("gx", "gy"), P("gx", "gy"), edge, edge)
        + (lists,) * 3
        + (P(),) * 11,
        out_specs=(P(None, "gx", "gy", None), edge),
        check_vma=False,
    )
```

```python
import functools
import math

import jax
import jax.numpy as jnp
from jax import lax
from jax.experimental import pallas as pl
from jax.experimental.pallas import tpu as pltpu
from jax.sharding import PartitionSpec as P

f32 = jnp.float32
bf16 = jnp.bfloat16

ATOMS = 128
EDGES = 512
CH = 64
LAT = 128
BASIS = 8
WIDTH = 2.5 / (BASIS - 1)
ROOT3 = math.sqrt(3.0)
DEGREE = (0, 1, 1, 1, 2, 2, 2, 2, 2)
STEPS = ((1, 0), (-1, 0), (0, 1), (0, -1), (1, 1), (1, -1), (-1, 1), (-1, -1))
FIRST_LANE = (0, 64, 0, 16, 32, 36, 40, 44)
LANES = (64, 64, 16, 16, 4, 4, 4, 4)
PACK_ONE = ((2, 72), (2, 72), (6, 24), (6, 24), (18, 8), (18, 8), (18, 8), (18, 8))
PACK_TWO = ((2, 288), (2, 288), (8, 72), (8, 72), (24, 24), (24, 24), (24, 24), (24, 24))


MEMBERS = (range(5), range(5, 9))
FARTHEST_FIRST = (4, 5, 6, 7, 0, 1, 2, 3)
FETCH_FIRST = (0, 1, 4, 5, 6)


def split(value):
    high = value.astype(bf16)
    return high, (value - high.astype(f32)).astype(bf16)


def mm(left, right):
    return jnp.dot(left, right, preferred_element_type=f32)


def side_by_side(value):
    return jnp.concatenate(split(value), axis=1)


def stacked(value):
    return jnp.concatenate(split(value), axis=0)


def weight_form(weight):
    high, low = split(weight)
    top = jnp.concatenate([high, high], axis=1)
    bottom = jnp.concatenate([low, jnp.zeros_like(low)], axis=1)
    return jnp.concatenate([top, bottom], axis=0)


def dense(form, stack):
    both = mm(form, stack)
    rows = both.shape[0] // 2
    return both[:rows] + both[rows:]


def iota(shape, axis):
    return lax.broadcasted_iota(jnp.int32, shape, axis)


def hot(mask):
    return jnp.where(mask, 1.0, 0.0).astype(bf16)


def rolled(value, shift):
    shift = shift % 128
    return value if shift == 0 else pltpu.roll(value, shift, 1)


def sigmoid_parts(value):
    gate = 1.0 / (1.0 + jnp.exp(-value))
    act = value * gate
    return act, gate + act * (1.0 - gate)


def body(
    grid,
    *refs,
):
    sources, (force_ref, energy_ref), scratch = refs[:20], refs[20:22], refs[22:]
    scratch = list(scratch)

    (
        pos_ref, feat_ref, centre_ref, neigh_ref, across_ref, along_ref, corner_ref, radial_ref,
        pair_ref, tensor_ref, gate1_ref, mix_ref, latent1_ref, gate2_ref, latent2_ref, readout_ref,
        vector_ref, self_ref, atom_count_ref, edge_count_ref, fetch_sem,
    ) = scratch[:21]
    fetches = [
        pltpu.make_async_copy(source, target, fetch_sem.at[i])
        for i, (source, target) in enumerate(zip(sources, scratch[:20]))
    ]
    del scratch[:21]

    def take(count):
        taken = scratch[:count]
        del scratch[:count]
        return taken

    out1, in1, out2, in2, out3, in3, in4 = (take(8) for _ in range(7))
    out4 = take(2)
    (
        hcn, hcnt, sel, selt, table1, table2, geo, lat, grads, big,
        g1, t1, joint, wide, mixed, pile, acc, env_own,
        pair_t, first_form, first_back, gate2_form, gate2_back, mix_form, mix_back, latent1_form,
        latent1_back, latent2_form, latent2_back, readout_form, readout_back, vector_col,
        radial_form, radial_back, gate_pair,
    ) = take(35)
    send_sem, recv_sem = take(2)

    def drow(m):
        return m * 8

    size_x, size_y = grid
    ix, iy = lax.axis_index("gx"), lax.axis_index("gy")

    along_x = {0: ix, 1: lax.rem(ix + 1, size_x), -1: lax.rem(ix + (size_x - 1), size_x)}
    along_y = {0: iy, 1: lax.rem(iy + 1, size_y), -1: lax.rem(iy + (size_y - 1), size_y)}

    def device(step, sign):
        return along_x[sign * step[0]], along_y[sign * step[1]]

    still = lax.div(ix, size_x)

    def lat_rows(first):
        return lat[pl.ds(pl.multiple_of(still * 8, 8) + first, 128)]

    barrier = pltpu.get_barrier_semaphore()
    for step in STEPS[::-1]:
        pl.semaphore_signal(
            barrier, inc=1, device_id=device(step, 1), device_id_type=pl.DeviceIdType.MESH
        )
    for i in FETCH_FIRST:
        fetches[i].start()
    for i in range(20):
        if i not in FETCH_FIRST:
            fetches[i].start()

    def copy(phase, k, source, target, sign, slot=None):
        slot = k if slot is None else slot
        return pltpu.make_async_remote_copy(
            src_ref=source,
            dst_ref=target,
            send_sem=send_sem.at[phase, slot],
            recv_sem=recv_sem.at[phase, slot],
            device_id=device(STEPS[k], sign),
            device_id_type=pl.DeviceIdType.MESH,
        )

    lane = iota((8, 128), 1)

    def pack(plan, k, table, target):
        groups, rows = plan[k]
        at = lane[:1]
        total = None
        for g in range(groups):
            piece = rolled(table[g * rows : (g + 1) * rows], LANES[k] * g - FIRST_LANE[k])
            total = piece if g == 0 else jnp.where(at >= LANES[k] * g, piece, total)
        target[...] = total

    def unpack_x(plan, ins):
        at = lane[:1]
        low, high = ins[0][...], ins[1][...]
        top = jnp.where(at < 64, low, rolled(high, 64))
        bottom = jnp.where(at < 64, rolled(low, 64), high)
        return jnp.concatenate([top, bottom], axis=0)

    def unpack_s(plan, ins):
        at = lane[:1]
        step = plan[4][1]
        pieces = []
        for b in range(plan[4][0]):
            value = None
            for k in range(2, 8):
                rows = plan[k][1]
                g, first = (b * step) // rows, (b * step) % rows
                piece = rolled(ins[k][first : first + step], FIRST_LANE[k] - LANES[k] * g)
                value = piece if k == 2 else jnp.where(at >= FIRST_LANE[k], piece, value)
            pieces.append(value)
        return jnp.concatenate(pieces, axis=0)

    for i in FETCH_FIRST:
        fetches[i].wait()

    def x_copies(phase, source, target, sign, chunk):
        rows = pl.ds(144 * chunk, 144)
        return [
            copy(phase, k, source[k].at[rows], target[k].at[rows], sign, k + 8 * chunk) for k in range(2)
        ]

    def pack_x(table, target, chunk):
        at = lane[:1]
        top, bottom = table[0:144], table[144:288]
        rows = slice(144 * chunk, 144 * chunk + 144)
        target[0][rows] = jnp.where(at < 64, top, rolled(bottom, 64))
        target[1][rows] = jnp.where(at < 64, rolled(top, 64), bottom)

    def unpack_x_chunk(ins, chunk):
        at = lane[:1]
        rows = slice(144 * chunk, 144 * chunk + 144)
        low, high = ins[0][rows], ins[1][rows]
        top = jnp.where(at < 64, low, rolled(high, 64))
        bottom = jnp.where(at < 64, rolled(low, 64), high)
        return jnp.concatenate([top, bottom], axis=0)

    half_rows = (slice(0, 288), slice(288, 576))

    across, along, corner = across_ref[0, 0], along_ref[0, 0], corner_ref[0, 0]
    list_x = jnp.concatenate([across[1:2], across[0:1]], axis=1)
    list_s = jnp.concatenate(
        [along[1:2], along[0:1], corner[3:4], corner[2:3], corner[1:2], corner[0:1],
         jnp.full((1, 80), -1, jnp.int32)],
        axis=1,
    )
    lists = jnp.concatenate([list_x, list_s], axis=1)
    chosen = hot(iota((128, 256), 0) == lists)
    sel[0:128] = chosen
    sel[128:256] = chosen

    sub8 = iota((8, 128), 0)
    features = feat_ref[0, 0]
    pos_own = jnp.where(
        sub8 == 0, pos_ref[0, 0],
        jnp.where(sub8 == 1, pos_ref[1, 0], jnp.where(sub8 == 2, pos_ref[2, 0], 0.0)),
    )
    pos_high = pos_own.astype(bf16).astype(f32)
    pos_mid = (pos_own - pos_high).astype(bf16).astype(f32)
    pos_low = pos_own - pos_high - pos_mid
    raw = side_by_side(jnp.concatenate([features, pos_own, pos_low], axis=0))
    sent = mm(raw, sel[...])
    sent = jnp.concatenate([sent[:128], sent[128:136] + sent[136:144], sent[136:144]], axis=0)
    for k in range(8):
        pack(PACK_ONE, k, sent[:, 0:128] if k < 2 else sent[:, 128:256], out1[k])

    pl.semaphore_wait(barrier, 8)
    first_copies = [copy(0, k, out1[k], in1[k], 1) for k in FARTHEST_FIRST]
    for one in first_copies:
        one.start()

    for i in (2, 3):
        fetches[i].wait()
    centre_row, neigh_row = centre_ref[0], neigh_ref[0]
    hot_c = hot(iota((128, EDGES), 0) == centre_row)
    hot_n = [hot(iota((128, EDGES), 0) + 128 * t == neigh_row) for t in range(3)]
    for t, value in enumerate([hot_c] + hot_n):
        hcn[256 * t : 256 * t + 128] = value
        hcn[256 * t + 128 : 256 * t + 256] = value
    centre_col = jnp.transpose(jnp.broadcast_to(centre_row.astype(f32), (128, EDGES)))
    neigh_col = jnp.transpose(jnp.broadcast_to(neigh_row.astype(f32), (128, EDGES)))
    lane_f = iota((1, 128), 1).astype(f32)
    hot_ct = hot(centre_col == lane_f)
    hot_nt = [hot(neigh_col == lane_f + 128.0 * t) for t in range(3)]
    for t, value in enumerate([hot_ct] + hot_nt):
        hcnt[0:EDGES, 128 * t : 128 * t + 128] = value
        hcnt[EDGES : 2 * EDGES, 128 * t : 128 * t + 128] = value
    selt_f = jnp.transpose(chosen.astype(f32)).astype(bf16)
    for t in range(2):
        selt[256 * t : 256 * t + 128] = selt_f[128 * t : 128 * t + 128]
        selt[256 * t + 128 : 256 * t + 256] = selt_f[128 * t : 128 * t + 128]

    def forward_form(weight):
        return weight_form(jnp.transpose(weight))

    def pair_form(first):
        both = jnp.transpose(first)
        high, low = split(both)
        low = jnp.where(iota((1, 128), 1) < 64, low.astype(f32), 0.0).astype(bf16)
        return jnp.concatenate([high, low], axis=0)

    for i in range(7, 20):
        fetches[i].wait()
    pair_t[...] = forward_form(pair_ref[1])
    own_raw = stacked(features)
    table1[:, 0:256] = side_by_side(dense(forward_form(pair_ref[0]), own_raw))
    table1[:, 256:512] = side_by_side(dense(pair_t[...], own_raw))
    self_rows = jnp.broadcast_to(self_ref[...].reshape(1, LAT), (16, LAT))
    self_row = dense(weight_form(self_rows), own_raw)[0:1]
    zeros64 = jnp.zeros((64, LAT), f32)
    first_t = jnp.concatenate([tensor_ref[...], gate1_ref[...]], axis=0)
    first_form[...] = weight_form(first_t)
    first_back[...] = forward_form(first_t)
    gate2_t = gate2_ref[...]
    gate2_form[...] = weight_form(gate2_t)
    gate2_back[...] = forward_form(jnp.concatenate([gate2_t, zeros64], axis=0))
    for d in range(3):
        weight = mix_ref[d]
        turned = jnp.transpose(weight)
        mix_form[d] = pair_form(jnp.concatenate([weight, weight], axis=0))
        mix_back[d] = pair_form(jnp.concatenate([turned, turned], axis=0))
    latent1_form[...] = forward_form(jnp.concatenate([latent1_ref[...], zeros64], axis=0))
    latent1_back[...] = weight_form(latent1_ref[...])
    latent2_form[...] = forward_form(jnp.concatenate([latent2_ref[...], zeros64], axis=0))
    latent2_back[...] = weight_form(latent2_ref[...])
    readout_form[...] = forward_form(readout_ref[...])
    readout_back[...] = weight_form(readout_ref[...])
    vector_col[...] = jnp.transpose(jnp.broadcast_to(vector_ref[...].reshape(1, LAT), (128, LAT)))
    radial_full = jnp.concatenate([radial_ref[...], jnp.zeros((120, LAT), f32)], axis=0)
    radial_form[...] = forward_form(radial_full)
    radial_back[...] = weight_form(radial_full[:16])

    lat[768:896] = mm(table1[:, 0:512], hcn[0:512])

    for one in first_copies:
        one.wait()
    table_x, table_s = unpack_x(PACK_ONE, in1), unpack_s(PACK_ONE, in1)
    ghost_raw = jnp.concatenate([table_x[:128], table_s[:128]], axis=1)
    ghost_proj = dense(pair_t[...], stacked(ghost_raw))
    table1[:, 512:768] = side_by_side(ghost_proj[:, 0:128])
    table1[:, 768:1024] = side_by_side(ghost_proj[:, 128:256])

    def offsets(rows):
        total = jnp.zeros((8, 128), f32)
        for k in rows:
            dx, dy = STEPS[k]
            inside = (lane >= FIRST_LANE[k]) & (lane < FIRST_LANE[k] + LANES[k])
            total = jnp.where(inside & (sub8 == 0), -1.0 * dx, total)
            total = jnp.where(inside & (sub8 == 1), -1.0 * dy, total)
        return total

    positions = jnp.concatenate(
        [pos_own, table_x[128:136] + offsets((0, 1)), table_s[128:136] + offsets(range(2, 8))], axis=1
    )
    p_high = positions.astype(bf16).astype(f32)
    p_mid = (positions - p_high).astype(bf16).astype(f32)
    p_low = positions - p_high - p_mid
    parts = jnp.concatenate([p_high, p_mid, p_low, jnp.zeros_like(p_low)], axis=0).astype(bf16)
    moved = mm(parts[:, 0:128], hcn[256:384] - hcn[0:128])
    moved += mm(parts[:, 128:256], hcn[512:640]) + mm(parts[:, 256:384], hcn[768:896])
    moved = moved[0:8] + moved[8:16] + moved[16:24]

    length = jnp.sqrt(jnp.sum(moved * moved, axis=0, keepdims=True) + 0.25)
    inverse = 1.0 / length
    unit = moved * inverse
    ux, uy, uz = unit[0:1], unit[1:2], unit[2:3]
    live = (iota((1, EDGES), 1) < edge_count_ref[...]).astype(f32)
    falloff = 1.0 / (1.0 + 0.25 * length * length)
    envelope = live * falloff
    square = ux * ux + uy * uy + uz * uz
    shapes = [
        jnp.ones_like(ux), ux, uy, uz, ROOT3 * ux * uy, ROOT3 * uy * uz,
        0.5 * (3.0 * uz * uz - square), ROOT3 * ux * uz, 0.5 * ROOT3 * (ux * ux - uy * uy),
    ]
    for m in range(9):
        geo[drow(m) : drow(m) + 8] = jnp.broadcast_to(shapes[m], (8, EDGES))
    geo[72:80] = jnp.broadcast_to(envelope, (8, EDGES))

    mid_points = 0.5 + WIDTH * iota((BASIS, EDGES), 0).astype(f32)
    scaled = (length - mid_points) / WIDTH
    basis = jnp.exp(-(scaled * scaled))
    basis_full = jnp.concatenate([basis, jnp.zeros((120, EDGES), f32)], axis=0)
    before0 = dense(radial_form[...], stacked(basis_full)) + lat_rows(768)
    before0 = before0 + mm(table1[:, 512:1024], hcn[512:1024])
    latent0, slope0 = sigmoid_parts(before0)
    lat[0:128] = slope0
    lat[128:256] = latent0
    high0, low0 = split(latent0)
    pile[0:128] = high0
    pile[384:512] = low0
    gains = dense(first_form[...], jnp.concatenate([high0, low0], axis=0))
    grads[0:128] = gains

    def lanes_at(t):
        return pl.ds(pl.multiple_of(t * 128, 128), 128)

    def shape_at(m, at):
        return geo[m * 8 : m * 8 + 1, at]

    def write_wide(row, t, value):
        high, low = split(value)
        wide[row : row + 16, lanes_at(t)] = high
        wide[row : row + 16, lanes_at(t + 4)] = low

    def spread(source, row0, members):
        def tile(t, carry):
            at = lanes_at(t)
            weight = 0.5 * geo[72:73, at]
            for c in range(4):
                gate = source[row0 + 16 * c : row0 + 16 * c + 16, at] * weight
                for m in members:
                    value = gate if m == 0 else gate * shape_at(m, at)
                    write_wide(64 * m + 16 * c, t, value)
            return carry

        lax.fori_loop(0, 4, tile, 0)

    second_x, sent = [], []
    second_copies = [copy(1, k, out2[k], in2[k], 1) for k in range(2, 8)]
    for c in range(2):
        spread(grads, 64, MEMBERS[c])
        env_pair = side_by_side(mm(wide[half_rows[c]], hcnt[:, 0:128]))
        table2[half_rows[c], 256:512] = env_pair
        sent.append(mm(env_pair, sel[...]))
        if c == 1:
            rest = jnp.concatenate([part[:, 128:256] for part in sent], axis=0)
            for k in (4, 5, 6, 7, 2, 3):
                pack(PACK_TWO, k, rest, out2[k])
                second_copies[k - 2].start()
        pack_x(sent[c][:, 0:128], out2, c)
        second_x.append(x_copies(1, out2, in2, 1, c))
        for one in second_x[c]:
            one.start()

    g1[...] = mm(table2[:, 256:512], hcn[0:256])

    def couple(t, carry):
        at = lanes_at(t)
        y = [None] + [shape_at(m, at) for m in range(1, 9)]
        for c in range(4):
            gain = grads[16 * c : 16 * c + 16, at]
            g = [g1[64 * m + 16 * c : 64 * m + 16 * c + 16, at] for m in range(9)]
            inner = [g[0] + g[0]] + [y[m] * g[0] + g[m] for m in range(1, 9)]
            inner[1] = inner[1] + (y[2] * g[3] - y[3] * g[2])
            inner[2] = inner[2] + (y[3] * g[1] - y[1] * g[3])
            inner[3] = inner[3] + (y[1] * g[2] - y[2] * g[1])
            for m in range(9):
                high, low = split(gain * inner[m])
                mixed[m, 16 * c : 16 * c + 16, at] = high
                mixed[m, 64 + 16 * c : 80 + 16 * c, at] = low
            sums = [
                g[0],
                y[1] * g[1] + y[2] * g[2] + y[3] * g[3],
                y[4] * g[4] + y[5] * g[5] + y[6] * g[6] + y[7] * g[7] + y[8] * g[8],
            ]
            for d in range(3):
                high, low = split(gain * sums[d])
                row = 128 + 64 * d + 16 * c
                pile[row : row + 16, at] = high
                pile[384 + row : 400 + row, at] = low
        return carry

    lax.fori_loop(0, 4, couple, 0)
    nothing = jnp.zeros((64, EDGES), bf16)
    pile[320:384] = nothing
    pile[704:768] = nothing
    act1, slope1 = sigmoid_parts(dense(latent1_form[...], pile[...]))
    lat[256:384] = slope1
    latent1 = lat_rows(128) + act1
    lat[384:512] = latent1
    high1, low1 = split(latent1)
    early = jnp.concatenate([latent2_form[:, 0:128], latent2_form[:, 384:512]], axis=1)
    lat[896:1024] = dense(early, jnp.concatenate([high1, low1], axis=0))
    grads[128:192] = dense(gate2_form[...], jnp.concatenate([high1, low1], axis=0))
    spread(grads, 128, range(9))
    table2[:, 0:256] = side_by_side(mm(wide[...], hcnt[:, 0:128]))
    joint[...] = mm(table2[...], hcn[0:512])
    for m in range(9):
        t1[64 * m : 64 * m + 64] = dense(mix_form[DEGREE[m]], mixed[m])

    for one in second_x[0]:
        one.wait()
    joint[0:288] += mm(side_by_side(unpack_x_chunk(in2, 0)), hcn[512:768])
    for one in second_copies:
        one.wait()
    joint[...] += mm(side_by_side(unpack_s(PACK_TWO, in2)), hcn[768:1024])

    def contract(degrees):
        def tile(t, carry):
            at = lanes_at(t)
            for c in range(4):
                for d in degrees:
                    total = None
                    for m in range(9):
                        if DEGREE[m] == d:
                            row = 64 * m + 16 * c
                            term = t1[row : row + 16, at] * joint[row : row + 16, at]
                            total = term if total is None else total + term
                    high, low = split(total)
                    row = 128 + 64 * d + 16 * c
                    pile[row : row + 16, at] = high
                    pile[384 + row : 400 + row, at] = low
            return carry

        lax.fori_loop(0, 4, tile, 0)

    contract((0, 1))
    for one in second_x[1]:
        one.wait()
    joint[288:576] += mm(side_by_side(unpack_x_chunk(in2, 1)), hcn[512:768])
    contract((2,))
    late = jnp.concatenate([latent2_form[:, 128:384], latent2_form[:, 512:768]], axis=1)
    late_pile = jnp.concatenate([pile[128:384], pile[512:768]], axis=0)
    act2, slope2 = sigmoid_parts(lat_rows(896) + dense(late, late_pile))
    latent2 = lat_rows(384) + act2
    hidden, slope_h = sigmoid_parts(dense(readout_form[...], stacked(latent2)))
    vector_wide = jnp.concatenate([vector_col[...]] * 4, axis=1)
    energy_raw = jnp.sum(vector_wide * hidden, axis=0, keepdims=True)
    edge_energy = envelope * energy_raw

    d_hidden = vector_wide * envelope * slope_h
    d_latent2 = dense(readout_back[...], stacked(d_hidden))
    d_pile = dense(latent2_back[...], stacked(d_latent2 * slope2))
    lat[512:640] = d_latent2 + d_pile[0:128]
    grads[192:384] = d_pile[128:320]

    def joint_back(members):
        def tile(t, carry):
            at = lanes_at(t)
            for c in range(4):
                d_sum = [grads[192 + 64 * d + 16 * c : 208 + 64 * d + 16 * c, at] for d in range(3)]
                for m in members:
                    row = 64 * m + 16 * c
                    write_wide(row, t, t1[row : row + 16, at] * d_sum[DEGREE[m]])
            return carry

        lax.fori_loop(0, 4, tile, 0)

    third_x, sent = [], []
    third_copies = [copy(2, k, out3[k], in3[k], -1) for k in range(2, 8)]
    for c in range(2):
        joint_back(MEMBERS[c])
        sent.append(mm(wide[half_rows[c]], hcnt[:, 256:512]))
        if c == 1:
            rest = jnp.concatenate([part[:, 128:256] for part in sent], axis=0)
            for k in (4, 5, 6, 7, 2, 3):
                pack(PACK_TWO, k, rest, out3[k])
                third_copies[k - 2].start()
        pack_x(sent[c][:, 0:128], out3, c)
        third_x.append(x_copies(2, out3, in3, -1, c))
        for one in third_x[c]:
            one.start()

    back = mm(wide[...], hcnt[:, 0:256])
    env_own[...] = back[:, 128:256]
    big[...] = mm(side_by_side(back[:, 0:128]), hcn[0:256])

    def mix_grads(t, carry):
        at = lanes_at(t)
        for c in range(4):
            d_sum = [grads[192 + 64 * d + 16 * c : 208 + 64 * d + 16 * c, at] for d in range(3)]
            for m in range(9):
                row = 64 * m + 16 * c
                high, low = split(joint[row : row + 16, at] * d_sum[DEGREE[m]])
                mixed[m, 16 * c : 16 * c + 16, at] = high
                mixed[m, 64 + 16 * c : 80 + 16 * c, at] = low
        return carry

    lax.fori_loop(0, 4, mix_grads, 0)
    for m in range(9):
        joint[64 * m : 64 * m + 64] = dense(mix_back[DEGREE[m]], mixed[m])

    def halves(value):
        return value[0:8] + value[8:16]

    def spread_back(source, row0, target0, fresh):
        def tile(t, carry):
            at = lanes_at(t)
            half = 0.5 * geo[72:73, at]
            d_shape = [None] * 9
            d_env = None
            for c in range(4):
                gate = source[row0 + 16 * c : row0 + 16 * c + 16, at]
                weight = gate * half
                total = None
                for m in range(9):
                    row = 64 * m + 16 * c
                    value = big[row : row + 16, at]
                    if m:
                        term = halves(value * weight)
                        d_shape[m] = term if c == 0 else d_shape[m] + term
                        value = value * shape_at(m, at)
                    total = value if m == 0 else total + value
                grads[target0 + 16 * c : target0 + 16 * c + 16, at] = total * half
                term = halves(total * gate)
                d_env = term if c == 0 else d_env + term
            d_env = 0.5 * d_env
            for m in range(1, 9):
                if fresh:
                    acc[drow(m) : drow(m) + 8, at] = d_shape[m]
                else:
                    acc[drow(m) : drow(m) + 8, at] += d_shape[m]
            if fresh:
                acc[0:8, at] = d_env
            else:
                acc[0:8, at] += d_env
            return carry

        lax.fori_loop(0, 4, tile, 0)

    spread_back(grads, 128, 384, True)
    gate_high, gate_low = split(grads[384:448])
    gate_pair[0:64] = gate_high
    gate_pair[64:128] = nothing
    gate_pair[128:192] = gate_low
    gate_pair[192:256] = nothing
    d_latent1 = lat_rows(512) + dense(gate2_back[...], gate_pair[...])
    d_pile = dense(latent1_back[...], stacked(d_latent1 * lat_rows(256)))
    lat[640:768] = d_latent1 + d_pile[0:128]
    grads[192:384] = d_pile[128:320]

    def couple_back(t, carry):
        at = lanes_at(t)
        y = [None] + [shape_at(m, at) for m in range(1, 9)]
        d_shape = [None] * 9
        for c in range(4):
            gain = grads[16 * c : 16 * c + 16, at]
            g = [g1[64 * m + 16 * c : 64 * m + 16 * c + 16, at] for m in range(9)]
            u = [joint[64 * m + 16 * c : 64 * m + 16 * c + 16, at] for m in range(9)]
            s = [grads[192 + 64 * d + 16 * c : 208 + 64 * d + 16 * c, at] for d in range(3)]
            inner = [g[0] + g[0]] + [y[m] * g[0] + g[m] for m in range(1, 9)]
            inner[1] = inner[1] + (y[2] * g[3] - y[3] * g[2])
            inner[2] = inner[2] + (y[3] * g[1] - y[1] * g[3])
            inner[3] = inner[3] + (y[1] * g[2] - y[2] * g[1])
            d_gain = s[0] * g[0]
            for m in range(9):
                d_gain = d_gain + u[m] * inner[m]
            d_gain = d_gain + s[1] * (y[1] * g[1] + y[2] * g[2] + y[3] * g[3])
            d_gain = d_gain + s[2] * (
                y[4] * g[4] + y[5] * g[5] + y[6] * g[6] + y[7] * g[7] + y[8] * g[8]
            )
            grads[448 + 16 * c : 464 + 16 * c, at] = d_gain
            k = [gain * value for value in u]
            q = [gain * value for value in s]
            d_g = [k[0] + k[0] + q[0]] + [k[m] + q[DEGREE[m]] * y[m] for m in range(1, 9)]
            for m in range(1, 9):
                d_g[0] = d_g[0] + k[m] * y[m]
            d_g[1] = d_g[1] + (k[2] * y[3] - k[3] * y[2])
            d_g[2] = d_g[2] + (k[3] * y[1] - k[1] * y[3])
            d_g[3] = d_g[3] + (k[1] * y[2] - k[2] * y[1])
            d_y = [None] + [k[m] * g[0] + q[DEGREE[m]] * g[m] for m in range(1, 9)]
            d_y[1] = d_y[1] + (k[3] * g[2] - k[2] * g[3])
            d_y[2] = d_y[2] + (k[1] * g[3] - k[3] * g[1])
            d_y[3] = d_y[3] + (k[2] * g[1] - k[1] * g[2])
            for m in range(1, 9):
                term = halves(d_y[m])
                d_shape[m] = term if c == 0 else d_shape[m] + term
            for m in range(9):
                write_wide(64 * m + 16 * c, t, d_g[m])
        for m in range(1, 9):
            acc[drow(m) : drow(m) + 8, at] += d_shape[m]
        return carry

    lax.fori_loop(0, 4, couple_back, 0)
    env_own[...] += mm(wide[...], hcnt[:, 0:128])

    for one in third_x[0]:
        one.wait()
    env_own[0:288] += mm(side_by_side(unpack_x_chunk(in3, 0)), selt[0:256])
    for one in third_copies:
        one.wait()
    env_own[...] += mm(side_by_side(unpack_s(PACK_TWO, in3)), selt[256:512])
    big[0:288] = mm(side_by_side(env_own[0:288]), hcn[0:256])
    for one in third_x[1]:
        one.wait()
    d_environment = env_own[288:576] + mm(side_by_side(unpack_x_chunk(in3, 1)), selt[0:256])
    big[288:576] = mm(side_by_side(d_environment), hcn[0:256])
    spread_back(grads, 64, 512, False)
    d_latent0 = lat_rows(640) + dense(first_back[...], stacked(grads[448:576]))
    d_basis = dense(radial_back[...], stacked(d_latent0 * lat_rows(0)))[:8]
    d_length = jnp.sum(d_basis * basis * scaled, axis=0, keepdims=True) * (-2.0 / WIDTH)
    d_env = jnp.sum(acc[0:8], axis=0, keepdims=True) + energy_raw
    d_length = d_length - 0.5 * length * envelope * falloff * d_env
    d_y = [None] + [jnp.sum(acc[drow(m) : drow(m) + 8], axis=0, keepdims=True) for m in range(1, 9)]
    d_ux = d_y[1] + ROOT3 * (uy * d_y[4] + uz * d_y[7] + ux * d_y[8]) - ux * d_y[6]
    d_uy = d_y[2] + ROOT3 * (ux * d_y[4] + uz * d_y[5] - uy * d_y[8]) - uy * d_y[6]
    d_uz = d_y[3] + ROOT3 * (uy * d_y[5] + ux * d_y[7]) + 2.0 * (uz * d_y[6])
    d_length = d_length - (d_ux * ux + d_uy * uy + d_uz * uz) * inverse
    sub_e = iota((8, EDGES), 0)
    d_unit = jnp.where(sub_e == 0, d_ux, jnp.where(sub_e == 1, d_uy, jnp.where(sub_e == 2, d_uz, 0.0)))
    d_moved = d_unit * inverse + d_length * unit

    def folded(value):
        high = value.astype(bf16).astype(f32)
        return jnp.concatenate([high, value - high], axis=0).astype(bf16)

    d_parts = folded(d_moved)
    d_table = halves(mm(d_parts, hcnt[0:EDGES, 128:512]))
    d_centre = halves(mm(d_parts, hcnt[0:EDGES, 0:128]))
    out4[0][...] = d_table[:, 128:256]
    out4[1][...] = d_table[:, 256:384]
    last_copies = [copy(3, k, out4[0] if k < 2 else out4[1], in4[k], -1) for k in FARTHEST_FIRST]
    for one in last_copies:
        one.start()
    d_own = d_table[:, 0:128] - d_centre

    per_atom = halves(mm(folded(jnp.broadcast_to(edge_energy, (8, EDGES))), hcnt[0:EDGES, 0:128]))[0:1]
    alive = (iota((1, ATOMS), 1) < atom_count_ref[...]).astype(f32)
    energy_ref[0] = alive * (per_atom + self_row)

    for one in last_copies:
        one.wait()
    grad_x = jnp.where(lane < 64, in4[0][...], in4[1][...])
    grad_s = in4[2][...]
    for k in range(3, 8):
        grad_s = jnp.where(lane >= FIRST_LANE[k], in4[k][...], grad_s)
    returned = mm(folded(grad_x), selt[0:128]) + mm(folded(grad_s), selt[256:384])
    total = d_own + halves(returned)
    for axis in range(3):
        force_ref[axis, 0] = -total[axis : axis + 1]


def per_device(grid, *args):
    args = list(args)
    for i in (11, 12, 15):
        args[i] = args[i].T
    sources = args[:2] + args[4:] + args[2:4]
    vmem = pl.BlockSpec(memory_space=pltpu.VMEM)
    specs = [pl.BlockSpec(memory_space=pltpu.HBM)] * 20
    packs = [
        [pltpu.VMEM((plan[k][1], 128), f32) for k in range(8)] for plan in (PACK_ONE, PACK_TWO)
    ]
    small = [pltpu.VMEM((8, 128), f32)]
    scratch = [pltpu.VMEM(source.shape, source.dtype) for source in sources]
    scratch += [pltpu.SemaphoreType.DMA((20,))]
    scratch += packs[0] * 2 + packs[1] * 4 + small * 8 + small * 2
    scratch += [
        pltpu.VMEM((1024, EDGES), bf16),
        pltpu.VMEM((2 * EDGES, 512), bf16),
        pltpu.VMEM((256, 256), bf16),
        pltpu.VMEM((512, 128), bf16),
        pltpu.VMEM((128, 1024), bf16),
        pltpu.VMEM((576, 512), bf16),
        pltpu.VMEM((80, EDGES), f32),
        pltpu.VMEM((1024, EDGES), f32),
        pltpu.VMEM((576, EDGES), f32),
        pltpu.VMEM((576, EDGES), f32),
        pltpu.VMEM((576, EDGES), f32),
        pltpu.VMEM((576, EDGES), f32),
        pltpu.VMEM((576, EDGES), f32),
        pltpu.VMEM((576, 2 * EDGES), bf16),
        pltpu.VMEM((9, 128, EDGES), bf16),
        pltpu.VMEM((768, EDGES), bf16),
        pltpu.VMEM((72, EDGES), f32),
        pltpu.VMEM((576, 128), f32),
        *(
            pltpu.VMEM(shape, bf16)
            for shape in (
                (256, 256), (256, 256), (256, 256), (128, 256), (256, 256), (3, 128, 128),
                (3, 128, 128), (256, 768), (640, 256), (256, 768), (640, 256), (256, 256), (256, 256),
            )
        ),
        pltpu.VMEM((128, 128), f32),
        pltpu.VMEM((256, 256), bf16),
        pltpu.VMEM((32, 256), bf16),
        pltpu.VMEM((256, EDGES), bf16),
        pltpu.SemaphoreType.DMA((4, 10)),
        pltpu.SemaphoreType.DMA((4, 10)),
    ]
    return pl.pallas_call(
        functools.partial(body, grid),
        out_shape=(
            jax.ShapeDtypeStruct((3, 1, 1, ATOMS), f32),
            jax.ShapeDtypeStruct((1, 1, ATOMS), f32),
        ),
        in_specs=specs,
        out_specs=(vmem, vmem),
        scratch_shapes=scratch,
        compiler_params=pltpu.CompilerParams(
            collective_id=0, has_side_effects=True, vmem_limit_bytes=64 * 1024 * 1024
        ),
    )(*sources)


def solution(mesh):
    grid = (mesh.shape["gx"], mesh.shape["gy"])
    edge = P("gx", "gy", None)
    lists = P("gx", "gy", None, None)
    return jax.shard_map(
        functools.partial(per_device, grid),
        mesh=mesh,
        in_specs=(P(None, "gx", "gy", None), lists, P("gx", "gy"), P("gx", "gy"), edge, edge)
        + (lists,) * 3
        + (P(),) * 11,
        out_specs=(P(None, "gx", "gy", None), edge),
        check_vma=False,
    )
```

```python
import functools
import math

import jax
import jax.numpy as jnp
from jax import lax
from jax.experimental import pallas as pl
from jax.experimental.pallas import tpu as pltpu
from jax.sharding import PartitionSpec as P

f32 = jnp.float32
bf16 = jnp.bfloat16

ATOMS = 128
EDGES = 512
CH = 64
LAT = 128
BASIS = 8
WIDTH = 2.5 / (BASIS - 1)
ROOT3 = math.sqrt(3.0)
DEGREE = (0, 1, 1, 1, 2, 2, 2, 2, 2)
STEPS = ((1, 0), (-1, 0), (0, 1), (0, -1), (1, 1), (1, -1), (-1, 1), (-1, -1))
FIRST_LANE = (0, 64, 0, 16, 32, 36, 40, 44)
LANES = (64, 64, 16, 16, 4, 4, 4, 4)
PACK_ONE = ((2, 72), (2, 72), (6, 24), (6, 24), (18, 8), (18, 8), (18, 8), (18, 8))
PACK_TWO = ((2, 288), (2, 288), (8, 72), (8, 72), (24, 24), (24, 24), (24, 24), (24, 24))


MEMBERS = (range(3), range(3, 6), range(6, 9))
FARTHEST_FIRST = (4, 5, 6, 7, 0, 1, 2, 3)
FETCH_FIRST = (0, 1, 8, 4, 5, 6)


def split(value):
    high = value.astype(bf16)
    return high, (value - high.astype(f32)).astype(bf16)


def mm(left, right):
    return jnp.dot(left, right, preferred_element_type=f32)


def side_by_side(value):
    return jnp.concatenate(split(value), axis=1)


def stacked(value):
    return jnp.concatenate(split(value), axis=0)


def weight_form(weight):
    high, low = split(weight)
    top = jnp.concatenate([high, high], axis=1)
    bottom = jnp.concatenate([low, jnp.zeros_like(low)], axis=1)
    return jnp.concatenate([top, bottom], axis=0)


def dense(form, stack):
    both = mm(form, stack)
    rows = both.shape[0] // 2
    return both[:rows] + both[rows:]


def iota(shape, axis):
    return lax.broadcasted_iota(jnp.int32, shape, axis)


def hot(mask):
    return jnp.where(mask, 1.0, 0.0).astype(bf16)


def rolled(value, shift):
    shift = shift % 128
    return value if shift == 0 else pltpu.roll(value, shift, 1)


def sigmoid_parts(value):
    gate = 1.0 / (1.0 + jnp.exp(-value))
    act = value * gate
    return act, gate + act * (1.0 - gate)


def body(
    grid,
    *refs,
):
    sources, out_ref, scratch = refs[:20], refs[20], refs[21:]
    scratch = list(scratch)

    (
        pos_ref, feat_ref, centre_ref, neigh_ref, across_ref, along_ref, corner_ref, radial_ref,
        pair_ref, tensor_ref, gate1_ref, mix_ref, latent1_ref, gate2_ref, latent2_ref, readout_ref,
        vector_ref, self_ref, atom_count_ref, edge_count_ref, fetch_sem,
    ) = scratch[:21]
    fetches = [
        pltpu.make_async_copy(source, target, fetch_sem.at[i])
        for i, (source, target) in enumerate(zip(sources, scratch[:20]))
    ]
    del scratch[:21]

    def take(count):
        taken = scratch[:count]
        del scratch[:count]
        return taken

    out1, in1, out2, in2, out3, in3, in4 = (take(8) for _ in range(7))
    out4 = take(2)
    (
        hcn, hcnt, sel, selt, table1, table2, geo, lat, grads, big,
        g1, t1, joint, wide, mixed, pile, acc, env_own,
        first_form, first_back, gate2_form, gate2_back, mix_form, mix_back, latent1_form,
        latent1_back, latent2_form, latent2_back, readout_form, readout_back, vector_col,
        radial_form, radial_back, gate_pair, pair2,
    ) = take(35)
    send_sem, recv_sem = take(2)

    def drow(m):
        return m * 8

    size_x, size_y = grid
    ix, iy = lax.axis_index("gx"), lax.axis_index("gy")

    along_x = {0: ix, 1: lax.rem(ix + 1, size_x), -1: lax.rem(ix + (size_x - 1), size_x)}
    along_y = {0: iy, 1: lax.rem(iy + 1, size_y), -1: lax.rem(iy + (size_y - 1), size_y)}

    def device(step, sign):
        return along_x[sign * step[0]], along_y[sign * step[1]]

    still = lax.div(ix, size_x)

    def lat_rows(first):
        return lat[pl.ds(pl.multiple_of(still * 8, 8) + first, 128)]

    barrier = pltpu.get_barrier_semaphore()
    for step in STEPS[::-1]:
        pl.semaphore_signal(
            barrier, inc=1, device_id=device(step, 1), device_id_type=pl.DeviceIdType.MESH
        )
    for i in FETCH_FIRST:
        fetches[i].start()
    for i in range(20):
        if i not in FETCH_FIRST:
            fetches[i].start()

    def copy(phase, k, source, target, sign, slot=None):
        slot = k if slot is None else slot
        return pltpu.make_async_remote_copy(
            src_ref=source,
            dst_ref=target,
            send_sem=send_sem.at[phase, slot],
            recv_sem=recv_sem.at[phase, slot],
            device_id=device(STEPS[k], sign),
            device_id_type=pl.DeviceIdType.MESH,
        )

    lane = iota((8, 128), 1)

    def pack(plan, k, table, target):
        groups, rows = plan[k]
        at = lane[:1]
        total = None
        for g in range(groups):
            piece = rolled(table[g * rows : (g + 1) * rows], LANES[k] * g - FIRST_LANE[k])
            total = piece if g == 0 else jnp.where(at >= LANES[k] * g, piece, total)
        target[...] = total

    def unpack_x(plan, ins):
        at = lane[:1]
        low, high = ins[0][...], ins[1][...]
        top = jnp.where(at < 64, low, rolled(high, 64))
        bottom = jnp.where(at < 64, rolled(low, 64), high)
        return jnp.concatenate([top, bottom], axis=0)

    def unpack_s(plan, ins):
        at = lane[:1]
        step = plan[4][1]
        pieces = []
        for b in range(plan[4][0]):
            value = None
            for k in range(2, 8):
                rows = plan[k][1]
                g, first = (b * step) // rows, (b * step) % rows
                piece = rolled(ins[k][first : first + step], FIRST_LANE[k] - LANES[k] * g)
                value = piece if k == 2 else jnp.where(at >= FIRST_LANE[k], piece, value)
            pieces.append(value)
        return jnp.concatenate(pieces, axis=0)

    for i in FETCH_FIRST:
        fetches[i].wait()

    def x_copies(phase, source, target, sign, chunk):
        rows = pl.ds(96 * chunk, 96)
        return [
            copy(phase, k, source[k].at[rows], target[k].at[rows], sign, k if chunk == 0 else 6 + k + 2 * chunk)
            for k in range(2)
        ]

    def pack_x(table, target, chunk):
        at = lane[:1]
        top, bottom = table[0:96], table[96:192]
        rows = slice(96 * chunk, 96 * chunk + 96)
        target[0][rows] = jnp.where(at < 64, top, rolled(bottom, 64))
        target[1][rows] = jnp.where(at < 64, rolled(top, 64), bottom)

    def unpack_x_chunk(ins, chunk):
        at = lane[:1]
        rows = slice(96 * chunk, 96 * chunk + 96)
        low, high = ins[0][rows], ins[1][rows]
        top = jnp.where(at < 64, low, rolled(high, 64))
        bottom = jnp.where(at < 64, rolled(low, 64), high)
        return jnp.concatenate([top, bottom], axis=0)

    third_rows = [slice(192 * c, 192 * c + 192) for c in range(3)]

    across, along, corner = across_ref[0, 0], along_ref[0, 0], corner_ref[0, 0]
    list_x = jnp.concatenate([across[1:2], across[0:1]], axis=1)
    list_s = jnp.concatenate(
        [along[1:2], along[0:1], corner[3:4], corner[2:3], corner[1:2], corner[0:1],
         jnp.full((1, 80), -1, jnp.int32)],
        axis=1,
    )
    lists = jnp.concatenate([list_x, list_s], axis=1)
    chosen = hot(iota((128, 256), 0) == lists)
    sel[0:128] = chosen
    sel[128:256] = chosen

    sub8 = iota((8, 128), 0)
    features = feat_ref[0, 0]
    pos_own = jnp.where(
        sub8 == 0, pos_ref[0, 0],
        jnp.where(sub8 == 1, pos_ref[1, 0], jnp.where(sub8 == 2, pos_ref[2, 0], 0.0)),
    )
    pos_high = pos_own.astype(bf16).astype(f32)
    pos_mid = (pos_own - pos_high).astype(bf16).astype(f32)
    pos_low = pos_own - pos_high - pos_mid
    own_raw = stacked(features)
    projected = dense(weight_form(jnp.transpose(pair_ref[1])), own_raw)
    raw = side_by_side(jnp.concatenate([projected, pos_own, pos_low], axis=0))
    sent = mm(raw, sel[...])
    sent = jnp.concatenate([sent[:128], sent[128:136] + sent[136:144], sent[136:144]], axis=0)
    for k in range(8):
        pack(PACK_ONE, k, sent[:, 0:128] if k < 2 else sent[:, 128:256], out1[k])

    pl.semaphore_wait(barrier, 8)
    first_copies = [copy(0, k, out1[k], in1[k], 1) for k in FARTHEST_FIRST]
    for one in first_copies:
        one.start()

    for i in (2, 3):
        fetches[i].wait()
    centre_row, neigh_row = centre_ref[0], neigh_ref[0]
    hot_c = hot(iota((128, EDGES), 0) == centre_row)
    hot_n = [hot(iota((128, EDGES), 0) + 128 * t == neigh_row) for t in range(3)]
    for t, value in enumerate([hot_c] + hot_n):
        hcn[256 * t : 256 * t + 128] = value
        hcn[256 * t + 128 : 256 * t + 256] = value
    centre_col = jnp.transpose(jnp.broadcast_to(centre_row.astype(f32), (128, EDGES)))
    neigh_col = jnp.transpose(jnp.broadcast_to(neigh_row.astype(f32), (128, EDGES)))
    lane_f = iota((1, 128), 1).astype(f32)
    hot_ct = hot(centre_col == lane_f)
    hot_nt = [hot(neigh_col == lane_f + 128.0 * t) for t in range(3)]
    for t, value in enumerate([hot_ct] + hot_nt):
        hcnt[0:EDGES, 128 * t : 128 * t + 128] = value
        hcnt[EDGES : 2 * EDGES, 128 * t : 128 * t + 128] = value
    selt_f = jnp.transpose(chosen.astype(f32)).astype(bf16)
    for t in range(2):
        selt[256 * t : 256 * t + 128] = selt_f[128 * t : 128 * t + 128]
        selt[256 * t + 128 : 256 * t + 256] = selt_f[128 * t : 128 * t + 128]

    def forward_form(weight):
        return weight_form(jnp.transpose(weight))

    def pair_form(first):
        both = jnp.transpose(first)
        high, low = split(both)
        low = jnp.where(iota((1, 128), 1) < 64, low.astype(f32), 0.0).astype(bf16)
        return jnp.concatenate([high, low], axis=0)

    for i in (7, *range(9, 20)):
        fetches[i].wait()
    table1[:, 0:256] = side_by_side(dense(forward_form(pair_ref[0]), own_raw))
    table1[:, 256:512] = side_by_side(projected)
    self_rows = jnp.broadcast_to(self_ref[...].reshape(1, LAT), (16, LAT))
    self_row = dense(weight_form(self_rows), own_raw)[0:1]
    zeros64 = jnp.zeros((64, LAT), f32)
    first_t = jnp.concatenate([tensor_ref[...], gate1_ref[...]], axis=0)
    first_form[...] = weight_form(first_t)
    first_back[...] = forward_form(first_t)
    gate2_t = gate2_ref[...]
    gate2_form[...] = weight_form(gate2_t)
    gate2_back[...] = forward_form(jnp.concatenate([gate2_t, zeros64], axis=0))
    for d in range(3):
        weight = mix_ref[d]
        turned = jnp.transpose(weight)
        mix_form[d] = pair_form(jnp.concatenate([weight, weight], axis=0))
        mix_back[d] = pair_form(jnp.concatenate([turned, turned], axis=0))
    latent1_form[...] = forward_form(jnp.concatenate([latent1_ref[...], zeros64], axis=0))
    latent1_back[...] = weight_form(latent1_ref[...])
    latent2_form[...] = forward_form(jnp.concatenate([latent2_ref[...], zeros64], axis=0))
    latent2_back[...] = weight_form(latent2_ref[...])
    readout_form[...] = forward_form(readout_ref[...])
    readout_back[...] = weight_form(readout_ref[...])
    vector_col[...] = jnp.transpose(jnp.broadcast_to(vector_ref[...].reshape(1, LAT), (128, LAT)))
    radial_full = jnp.concatenate([radial_ref[...], jnp.zeros((120, LAT), f32)], axis=0)
    radial_form[...] = forward_form(radial_full)
    radial_back[...] = weight_form(radial_full[:16])

    lat[768:896] = mm(table1[:, 0:512], hcn[0:512])

    for one in first_copies:
        one.wait()
    table_x, table_s = unpack_x(PACK_ONE, in1), unpack_s(PACK_ONE, in1)
    table1[:, 512:768] = side_by_side(table_x[:128])
    table1[:, 768:1024] = side_by_side(table_s[:128])

    def offsets(rows):
        total = jnp.zeros((8, 128), f32)
        for k in rows:
            dx, dy = STEPS[k]
            inside = (lane >= FIRST_LANE[k]) & (lane < FIRST_LANE[k] + LANES[k])
            total = jnp.where(inside & (sub8 == 0), -1.0 * dx, total)
            total = jnp.where(inside & (sub8 == 1), -1.0 * dy, total)
        return total

    positions = jnp.concatenate(
        [pos_own, table_x[128:136] + offsets((0, 1)), table_s[128:136] + offsets(range(2, 8))], axis=1
    )
    p_high = positions.astype(bf16).astype(f32)
    p_mid = (positions - p_high).astype(bf16).astype(f32)
    p_low = positions - p_high - p_mid
    parts = jnp.concatenate([p_high, p_mid, p_low, jnp.zeros_like(p_low)], axis=0).astype(bf16)
    moved = mm(parts[:, 0:128], hcn[256:384] - hcn[0:128])
    moved += mm(parts[:, 128:256], hcn[512:640]) + mm(parts[:, 256:384], hcn[768:896])
    moved = moved[0:8] + moved[8:16] + moved[16:24]

    length = jnp.sqrt(jnp.sum(moved * moved, axis=0, keepdims=True) + 0.25)
    inverse = 1.0 / length
    unit = moved * inverse
    ux, uy, uz = unit[0:1], unit[1:2], unit[2:3]
    live = (iota((1, EDGES), 1) < edge_count_ref[...]).astype(f32)
    falloff = 1.0 / (1.0 + 0.25 * length * length)
    envelope = live * falloff
    square = ux * ux + uy * uy + uz * uz
    shapes = [
        jnp.ones_like(ux), ux, uy, uz, ROOT3 * ux * uy, ROOT3 * uy * uz,
        0.5 * (3.0 * uz * uz - square), ROOT3 * ux * uz, 0.5 * ROOT3 * (ux * ux - uy * uy),
    ]
    for m in range(9):
        geo[drow(m) : drow(m) + 8] = jnp.broadcast_to(shapes[m], (8, EDGES))
    geo[72:80] = jnp.broadcast_to(envelope, (8, EDGES))

    mid_points = 0.5 + WIDTH * iota((BASIS, EDGES), 0).astype(f32)
    scaled = (length - mid_points) / WIDTH
    basis = jnp.exp(-(scaled * scaled))
    basis_full = jnp.concatenate([basis, jnp.zeros((120, EDGES), f32)], axis=0)
    before0 = dense(radial_form[...], stacked(basis_full)) + lat_rows(768)
    before0 = before0 + mm(table1[:, 512:1024], hcn[512:1024])
    latent0, slope0 = sigmoid_parts(before0)
    lat[0:128] = slope0
    lat[128:256] = latent0
    high0, low0 = split(latent0)
    pile[0:128] = high0
    pile[384:512] = low0
    gains = dense(first_form[...], jnp.concatenate([high0, low0], axis=0))
    grads[0:128] = gains

    def lanes_at(t):
        return pl.ds(pl.multiple_of(t * 128, 128), 128)

    def shape_at(m, at):
        return geo[m * 8 : m * 8 + 1, at]

    def write_wide(row, t, value):
        high, low = split(value)
        wide[row : row + 16, lanes_at(t)] = high
        wide[row : row + 16, lanes_at(t + 4)] = low

    def spread(source, row0, members):
        def tile(t, carry):
            at = lanes_at(t)
            weight = 0.5 * geo[72:73, at]
            for c in range(4):
                gate = source[row0 + 16 * c : row0 + 16 * c + 16, at] * weight
                for m in members:
                    value = gate if m == 0 else gate * shape_at(m, at)
                    write_wide(64 * m + 16 * c, t, value)
            return carry

        lax.fori_loop(0, 4, tile, 0)

    second_x, sent = [], []
    second_copies = [copy(1, k, out2[k], in2[k], 1) for k in range(2, 8)]
    for c in range(3):
        spread(grads, 64, MEMBERS[c])
        env_pair = side_by_side(mm(wide[third_rows[c]], hcnt[:, 0:128]))
        table2[third_rows[c], 256:512] = env_pair
        sent.append(mm(env_pair, sel[...]))
        if c == 2:
            rest = jnp.concatenate([part[:, 128:256] for part in sent], axis=0)
            for k in (4, 5, 6, 7, 2, 3):
                pack(PACK_TWO, k, rest, out2[k])
                second_copies[k - 2].start()
        pack_x(sent[c][:, 0:128], out2, c)
        second_x.append(x_copies(1, out2, in2, 1, c))
        for one in second_x[c]:
            one.start()

    g1[...] = mm(table2[:, 256:512], hcn[0:256])

    def couple(t, carry):
        at = lanes_at(t)
        y = [None] + [shape_at(m, at) for m in range(1, 9)]
        for c in range(4):
            gain = grads[16 * c : 16 * c + 16, at]
            g = [g1[64 * m + 16 * c : 64 * m + 16 * c + 16, at] for m in range(9)]
            inner = [g[0] + g[0]] + [y[m] * g[0] + g[m] for m in range(1, 9)]
            inner[1] = inner[1] + (y[2] * g[3] - y[3] * g[2])
            inner[2] = inner[2] + (y[3] * g[1] - y[1] * g[3])
            inner[3] = inner[3] + (y[1] * g[2] - y[2] * g[1])
            for m in range(9):
                high, low = split(gain * inner[m])
                mixed[m, 16 * c : 16 * c + 16, at] = high
                mixed[m, 64 + 16 * c : 80 + 16 * c, at] = low
            sums = [
                g[0],
                y[1] * g[1] + y[2] * g[2] + y[3] * g[3],
                y[4] * g[4] + y[5] * g[5] + y[6] * g[6] + y[7] * g[7] + y[8] * g[8],
            ]
            for d in range(3):
                high, low = split(gain * sums[d])
                row = 128 + 64 * d + 16 * c
                pile[row : row + 16, at] = high
                pile[384 + row : 400 + row, at] = low
        return carry

    lax.fori_loop(0, 4, couple, 0)
    nothing = jnp.zeros((64, EDGES), bf16)
    pile[320:384] = nothing
    pile[704:768] = nothing
    act1, slope1 = sigmoid_parts(dense(latent1_form[...], pile[...]))
    lat[256:384] = slope1
    latent1 = lat_rows(128) + act1
    lat[384:512] = latent1
    high1, low1 = split(latent1)
    early = jnp.concatenate([latent2_form[:, 0:128], latent2_form[:, 384:512]], axis=1)
    lat[896:1024] = dense(early, jnp.concatenate([high1, low1], axis=0))
    grads[128:192] = dense(gate2_form[...], jnp.concatenate([high1, low1], axis=0))
    spread(grads, 128, range(9))
    table2[:, 0:256] = side_by_side(mm(wide[...], hcnt[:, 0:128]))
    joint[...] = mm(table2[...], hcn[0:512])
    for m in range(9):
        t1[64 * m : 64 * m + 64] = dense(mix_form[DEGREE[m]], mixed[m])

    for c in range(2):
        for one in second_x[c]:
            one.wait()
        joint[third_rows[c]] += mm(side_by_side(unpack_x_chunk(in2, c)), hcn[512:768])
    for one in second_copies:
        one.wait()
    joint[...] += mm(side_by_side(unpack_s(PACK_TWO, in2)), hcn[768:1024])

    def contract(degrees):
        def tile(t, carry):
            at = lanes_at(t)
            for c in range(4):
                for d in degrees:
                    total = None
                    for m in range(9):
                        if DEGREE[m] == d:
                            row = 64 * m + 16 * c
                            term = t1[row : row + 16, at] * joint[row : row + 16, at]
                            total = term if total is None else total + term
                    high, low = split(total)
                    row = 128 + 64 * d + 16 * c
                    pile[row : row + 16, at] = high
                    pile[384 + row : 400 + row, at] = low
            return carry

        lax.fori_loop(0, 4, tile, 0)

    contract((0, 1))
    for one in second_x[2]:
        one.wait()
    joint[384:576] += mm(side_by_side(unpack_x_chunk(in2, 2)), hcn[512:768])
    contract((2,))
    late = jnp.concatenate([latent2_form[:, 128:384], latent2_form[:, 512:768]], axis=1)
    late_pile = jnp.concatenate([pile[128:384], pile[512:768]], axis=0)
    act2, slope2 = sigmoid_parts(lat_rows(896) + dense(late, late_pile))
    latent2 = lat_rows(384) + act2
    hidden, slope_h = sigmoid_parts(dense(readout_form[...], stacked(latent2)))
    vector_wide = jnp.concatenate([vector_col[...]] * 4, axis=1)
    energy_raw = jnp.sum(vector_wide * hidden, axis=0, keepdims=True)
    edge_energy = envelope * energy_raw

    d_hidden = vector_wide * envelope * slope_h
    d_latent2 = dense(readout_back[...], stacked(d_hidden))
    d_before2 = stacked(d_latent2 * slope2)
    grads[192:384] = mm(latent2_back[128:320], d_before2) + mm(latent2_back[448:640], d_before2)
    lat[512:640] = d_latent2
    pair2[...] = d_before2

    def joint_back(members):
        def tile(t, carry):
            at = lanes_at(t)
            for c in range(4):
                d_sum = [grads[192 + 64 * d + 16 * c : 208 + 64 * d + 16 * c, at] for d in range(3)]
                for m in members:
                    row = 64 * m + 16 * c
                    write_wide(row, t, t1[row : row + 16, at] * d_sum[DEGREE[m]])
            return carry

        lax.fori_loop(0, 4, tile, 0)

    third_x, sent = [], []
    third_copies = [copy(2, k, out3[k], in3[k], -1) for k in range(2, 8)]
    for c in range(3):
        joint_back(MEMBERS[c])
        sent.append(mm(wide[third_rows[c]], hcnt[:, 256:512]))
        if c == 2:
            rest = jnp.concatenate([part[:, 128:256] for part in sent], axis=0)
            for k in (4, 5, 6, 7, 2, 3):
                pack(PACK_TWO, k, rest, out3[k])
                third_copies[k - 2].start()
        pack_x(sent[c][:, 0:128], out3, c)
        third_x.append(x_copies(2, out3, in3, -1, c))
        for one in third_x[c]:
            one.start()

    both = mm(latent2_back[0:128], pair2[...]) + mm(latent2_back[320:448], pair2[...])
    lat[512:640] = lat_rows(512) + both
    back = mm(wide[...], hcnt[:, 0:256])
    env_own[...] = back[:, 128:256]
    big[...] = mm(side_by_side(back[:, 0:128]), hcn[0:256])

    def mix_grads(t, carry):
        at = lanes_at(t)
        for c in range(4):
            d_sum = [grads[192 + 64 * d + 16 * c : 208 + 64 * d + 16 * c, at] for d in range(3)]
            for m in range(9):
                row = 64 * m + 16 * c
                high, low = split(joint[row : row + 16, at] * d_sum[DEGREE[m]])
                mixed[m, 16 * c : 16 * c + 16, at] = high
                mixed[m, 64 + 16 * c : 80 + 16 * c, at] = low
        return carry

    lax.fori_loop(0, 4, mix_grads, 0)
    for m in range(9):
        joint[64 * m : 64 * m + 64] = dense(mix_back[DEGREE[m]], mixed[m])

    def halves(value):
        return value[0:8] + value[8:16]

    def spread_back(source, row0, target0, members, fresh, first, last):
        def tile(t, carry):
            at = lanes_at(t)
            half = 0.5 * geo[72:73, at]
            d_shape = [None] * 9
            d_env = None
            for c in range(4):
                gate = source[row0 + 16 * c : row0 + 16 * c + 16, at]
                weight = gate * half
                total = None if first else grads[target0 + 16 * c : target0 + 16 * c + 16, at]
                for m in members:
                    row = 64 * m + 16 * c
                    value = big[row : row + 16, at]
                    if m:
                        term = halves(value * weight)
                        d_shape[m] = term if c == 0 else d_shape[m] + term
                        value = value * shape_at(m, at)
                    total = value if total is None else total + value
                if last:
                    term = halves(total * gate)
                    d_env = term if c == 0 else d_env + term
                    total = total * half
                grads[target0 + 16 * c : target0 + 16 * c + 16, at] = total
            for m in members:
                if m and fresh:
                    acc[drow(m) : drow(m) + 8, at] = d_shape[m]
                elif m:
                    acc[drow(m) : drow(m) + 8, at] += d_shape[m]
            if last and fresh:
                acc[0:8, at] = 0.5 * d_env
            elif last:
                acc[0:8, at] += 0.5 * d_env
            return carry

        lax.fori_loop(0, 4, tile, 0)

    spread_back(grads, 128, 384, range(9), True, True, True)
    gate_high, gate_low = split(grads[384:448])
    gate_pair[0:64] = gate_high
    gate_pair[64:128] = nothing
    gate_pair[128:192] = gate_low
    gate_pair[192:256] = nothing
    d_latent1 = lat_rows(512) + dense(gate2_back[...], gate_pair[...])
    d_pile = dense(latent1_back[...], stacked(d_latent1 * lat_rows(256)))
    lat[640:768] = d_latent1 + d_pile[0:128]
    grads[192:384] = d_pile[128:320]

    def couple_back(t, carry):
        at = lanes_at(t)
        y = [None] + [shape_at(m, at) for m in range(1, 9)]
        d_shape = [None] * 9
        for c in range(4):
            gain = grads[16 * c : 16 * c + 16, at]
            g = [g1[64 * m + 16 * c : 64 * m + 16 * c + 16, at] for m in range(9)]
            u = [joint[64 * m + 16 * c : 64 * m + 16 * c + 16, at] for m in range(9)]
            s = [grads[192 + 64 * d + 16 * c : 208 + 64 * d + 16 * c, at] for d in range(3)]
            inner = [g[0] + g[0]] + [y[m] * g[0] + g[m] for m in range(1, 9)]
            inner[1] = inner[1] + (y[2] * g[3] - y[3] * g[2])
            inner[2] = inner[2] + (y[3] * g[1] - y[1] * g[3])
            inner[3] = inner[3] + (y[1] * g[2] - y[2] * g[1])
            d_gain = s[0] * g[0]
            for m in range(9):
                d_gain = d_gain + u[m] * inner[m]
            d_gain = d_gain + s[1] * (y[1] * g[1] + y[2] * g[2] + y[3] * g[3])
            d_gain = d_gain + s[2] * (
                y[4] * g[4] + y[5] * g[5] + y[6] * g[6] + y[7] * g[7] + y[8] * g[8]
            )
            grads[448 + 16 * c : 464 + 16 * c, at] = d_gain
            k = [gain * value for value in u]
            q = [gain * value for value in s]
            d_g = [k[0] + k[0] + q[0]] + [k[m] + q[DEGREE[m]] * y[m] for m in range(1, 9)]
            for m in range(1, 9):
                d_g[0] = d_g[0] + k[m] * y[m]
            d_g[1] = d_g[1] + (k[2] * y[3] - k[3] * y[2])
            d_g[2] = d_g[2] + (k[3] * y[1] - k[1] * y[3])
            d_g[3] = d_g[3] + (k[1] * y[2] - k[2] * y[1])
            d_y = [None] + [k[m] * g[0] + q[DEGREE[m]] * g[m] for m in range(1, 9)]
            d_y[1] = d_y[1] + (k[3] * g[2] - k[2] * g[3])
            d_y[2] = d_y[2] + (k[1] * g[3] - k[3] * g[1])
            d_y[3] = d_y[3] + (k[2] * g[1] - k[1] * g[2])
            for m in range(1, 9):
                term = halves(d_y[m])
                d_shape[m] = term if c == 0 else d_shape[m] + term
            for m in range(9):
                write_wide(64 * m + 16 * c, t, d_g[m])
        for m in range(1, 9):
            acc[drow(m) : drow(m) + 8, at] += d_shape[m]
        return carry

    lax.fori_loop(0, 4, couple_back, 0)
    env_own[...] += mm(wide[...], hcnt[:, 0:128])

    for c in range(2):
        for one in third_x[c]:
            one.wait()
        env_own[third_rows[c]] += mm(side_by_side(unpack_x_chunk(in3, c)), selt[0:256])
    for one in third_copies:
        one.wait()
    env_own[...] += mm(side_by_side(unpack_s(PACK_TWO, in3)), selt[256:512])
    big[0:384] = mm(side_by_side(env_own[0:384]), hcn[0:256])
    spread_back(grads, 64, 512, range(6), False, True, False)
    for one in third_x[2]:
        one.wait()
    d_environment = env_own[384:576] + mm(side_by_side(unpack_x_chunk(in3, 2)), selt[0:256])
    big[384:576] = mm(side_by_side(d_environment), hcn[0:256])
    spread_back(grads, 64, 512, range(6, 9), False, False, True)
    d_latent0 = lat_rows(640) + dense(first_back[...], stacked(grads[448:576]))
    d_basis = dense(radial_back[...], stacked(d_latent0 * lat_rows(0)))[:8]
    d_length = jnp.sum(d_basis * basis * scaled, axis=0, keepdims=True) * (-2.0 / WIDTH)
    d_env = jnp.sum(acc[0:8], axis=0, keepdims=True) + energy_raw
    d_length = d_length - 0.5 * length * envelope * falloff * d_env
    d_y = [None] + [jnp.sum(acc[drow(m) : drow(m) + 8], axis=0, keepdims=True) for m in range(1, 9)]
    d_ux = d_y[1] + ROOT3 * (uy * d_y[4] + uz * d_y[7] + ux * d_y[8]) - ux * d_y[6]
    d_uy = d_y[2] + ROOT3 * (ux * d_y[4] + uz * d_y[5] - uy * d_y[8]) - uy * d_y[6]
    d_uz = d_y[3] + ROOT3 * (uy * d_y[5] + ux * d_y[7]) + 2.0 * (uz * d_y[6])
    d_length = d_length - (d_ux * ux + d_uy * uy + d_uz * uz) * inverse
    sub_e = iota((8, EDGES), 0)
    d_unit = jnp.where(sub_e == 0, d_ux, jnp.where(sub_e == 1, d_uy, jnp.where(sub_e == 2, d_uz, 0.0)))
    d_moved = d_unit * inverse + d_length * unit

    def folded(value):
        high = value.astype(bf16).astype(f32)
        return jnp.concatenate([high, value - high], axis=0).astype(bf16)

    d_parts = folded(d_moved)
    d_table = halves(mm(d_parts, hcnt[0:EDGES, 128:512]))
    d_centre = halves(mm(d_parts, hcnt[0:EDGES, 0:128]))
    out4[0][...] = d_table[:, 128:256]
    out4[1][...] = d_table[:, 256:384]
    last_copies = [copy(3, k, out4[0] if k < 2 else out4[1], in4[k], -1) for k in FARTHEST_FIRST]
    for one in last_copies:
        one.start()
    d_own = d_table[:, 0:128] - d_centre

    per_atom = halves(mm(folded(jnp.broadcast_to(edge_energy, (8, EDGES))), hcnt[0:EDGES, 0:128]))[0:1]
    alive = (iota((1, ATOMS), 1) < atom_count_ref[...]).astype(f32)
    out_ref[3, 0] = -(alive * (per_atom + self_row))

    for one in last_copies:
        one.wait()
    grad_x = jnp.where(lane < 64, in4[0][...], in4[1][...])
    grad_s = in4[2][...]
    for k in range(3, 8):
        grad_s = jnp.where(lane >= FIRST_LANE[k], in4[k][...], grad_s)
    returned = mm(folded(grad_x), selt[0:128]) + mm(folded(grad_s), selt[256:384])
    total = d_own + halves(returned)
    for axis in range(3):
        out_ref[axis, 0] = total[axis : axis + 1]


def per_device(grid, *args):
    args = list(args)
    for i in (11, 12, 15):
        args[i] = args[i].T
    sources = args[:2] + args[4:] + args[2:4]
    vmem = pl.BlockSpec(memory_space=pltpu.VMEM)
    specs = [pl.BlockSpec(memory_space=pltpu.HBM)] * 20
    packs = [
        [pltpu.VMEM((plan[k][1], 128), f32) for k in range(8)] for plan in (PACK_ONE, PACK_TWO)
    ]
    small = [pltpu.VMEM((8, 128), f32)]
    scratch = [pltpu.VMEM(source.shape, source.dtype) for source in sources]
    scratch += [pltpu.SemaphoreType.DMA((20,))]
    scratch += packs[0] * 2 + packs[1] * 4 + small * 8 + small * 2
    scratch += [
        pltpu.VMEM((1024, EDGES), bf16),
        pltpu.VMEM((2 * EDGES, 512), bf16),
        pltpu.VMEM((256, 256), bf16),
        pltpu.VMEM((512, 128), bf16),
        pltpu.VMEM((128, 1024), bf16),
        pltpu.VMEM((576, 512), bf16),
        pltpu.VMEM((80, EDGES), f32),
        pltpu.VMEM((1024, EDGES), f32),
        pltpu.VMEM((576, EDGES), f32),
        pltpu.VMEM((576, EDGES), f32),
        pltpu.VMEM((576, EDGES), f32),
        pltpu.VMEM((576, EDGES), f32),
        pltpu.VMEM((576, EDGES), f32),
        pltpu.VMEM((576, 2 * EDGES), bf16),
        pltpu.VMEM((9, 128, EDGES), bf16),
        pltpu.VMEM((768, EDGES), bf16),
        pltpu.VMEM((72, EDGES), f32),
        pltpu.VMEM((576, 128), f32),
        *(
            pltpu.VMEM(shape, bf16)
            for shape in (
                (256, 256), (256, 256), (128, 256), (256, 256), (3, 128, 128),
                (3, 128, 128), (256, 768), (640, 256), (256, 768), (640, 256), (256, 256), (256, 256),
            )
        ),
        pltpu.VMEM((128, 128), f32),
        pltpu.VMEM((256, 256), bf16),
        pltpu.VMEM((32, 256), bf16),
        pltpu.VMEM((256, EDGES), bf16),
        pltpu.VMEM((256, EDGES), bf16),
        pltpu.SemaphoreType.DMA((4, 12)),
        pltpu.SemaphoreType.DMA((4, 12)),
    ]
    result = pl.pallas_call(
        functools.partial(body, grid),
        out_shape=jax.ShapeDtypeStruct((4, 1, 1, ATOMS), f32),
        in_specs=specs,
        out_specs=vmem,
        scratch_shapes=scratch,
        compiler_params=pltpu.CompilerParams(
            collective_id=0, has_side_effects=True, vmem_limit_bytes=64 * 1024 * 1024
        ),
    )(*sources)
    result = -result
    return result[:3], result[3]


def solution(mesh):
    grid = (mesh.shape["gx"], mesh.shape["gy"])
    edge = P("gx", "gy", None)
    lists = P("gx", "gy", None, None)
    return jax.shard_map(
        functools.partial(per_device, grid),
        mesh=mesh,
        in_specs=(P(None, "gx", "gy", None), lists, P("gx", "gy"), P("gx", "gy"), edge, edge)
        + (lists,) * 3
        + (P(),) * 11,
        out_specs=(P(None, "gx", "gy", None), edge),
        check_vma=False,
    )
```

```python
import functools
import math

import jax
import jax.numpy as jnp
from jax import lax
from jax.experimental import pallas as pl
from jax.experimental.pallas import tpu as pltpu
from jax.sharding import PartitionSpec as P

f32 = jnp.float32
bf16 = jnp.bfloat16

ATOMS = 128
EDGES = 512
CH = 64
LAT = 128
BASIS = 8
WIDTH = 2.5 / (BASIS - 1)
ROOT3 = math.sqrt(3.0)
DEGREE = (0, 1, 1, 1, 2, 2, 2, 2, 2)
STEPS = ((1, 0), (-1, 0), (0, 1), (0, -1), (1, 1), (1, -1), (-1, 1), (-1, -1))
FIRST_LANE = (0, 64, 0, 16, 32, 36, 40, 44)
LANES = (64, 64, 16, 16, 4, 4, 4, 4)
PACK_ONE = ((2, 72), (2, 72), (6, 24), (6, 24), (18, 8), (18, 8), (18, 8), (18, 8))
PACK_TWO = ((2, 288), (2, 288), (8, 72), (8, 72), (24, 24), (24, 24), (24, 24), (24, 24))


MEMBERS = (range(3), range(3, 6), range(6, 9))
FARTHEST_FIRST = (4, 5, 6, 7, 0, 1, 2, 3)
FETCH_FIRST = (0, 1, 8, 4, 5, 6)


def split(value):
    high = value.astype(bf16)
    return high, (value - high.astype(f32)).astype(bf16)


def mm(left, right):
    return jnp.dot(left, right, preferred_element_type=f32)


def side_by_side(value):
    return jnp.concatenate(split(value), axis=1)


def stacked(value):
    return jnp.concatenate(split(value), axis=0)


def weight_form(weight):
    high, low = split(weight)
    top = jnp.concatenate([high, high], axis=1)
    bottom = jnp.concatenate([low, jnp.zeros_like(low)], axis=1)
    return jnp.concatenate([top, bottom], axis=0)


def dense(form, stack):
    both = mm(form, stack)
    rows = both.shape[0] // 2
    return both[:rows] + both[rows:]


def iota(shape, axis):
    return lax.broadcasted_iota(jnp.int32, shape, axis)


def hot(mask):
    return jnp.where(mask, 1.0, 0.0).astype(bf16)


def rolled(value, shift):
    shift = shift % 128
    return value if shift == 0 else pltpu.roll(value, shift, 1)


def sigmoid_parts(value):
    gate = 1.0 / (1.0 + jnp.exp(-value))
    act = value * gate
    return act, gate + act * (1.0 - gate)


def body(
    grid,
    *refs,
):
    sources, out_ref, scratch = refs[:20], refs[20], refs[21:]
    scratch = list(scratch)

    (
        pos_ref, feat_ref, centre_ref, neigh_ref, across_ref, along_ref, corner_ref, radial_ref,
        pair_ref, tensor_ref, gate1_ref, mix_ref, latent1_ref, gate2_ref, latent2_ref, readout_ref,
        vector_ref, self_ref, atom_count_ref, edge_count_ref, fetch_sem,
    ) = scratch[:21]
    fetches = [
        pltpu.make_async_copy(source, target, fetch_sem.at[i])
        for i, (source, target) in enumerate(zip(sources, scratch[:20]))
    ]
    del scratch[:21]

    def take(count):
        taken = scratch[:count]
        del scratch[:count]
        return taken

    out1, in1, out2, in2, out3, in3, in4 = (take(8) for _ in range(7))
    out4 = take(2)
    (
        hcn, hcnt, sel, selt, table1, table2, geo, lat, grads, big,
        g1, t1, joint, wide, mixed, pile, acc, env_own,
        first_form, first_back, gate2_form, gate2_back, mix_form, mix_back, latent1_form,
        latent1_back, latent2_form, latent2_back, readout_form, readout_back, vector_col,
        radial_form, radial_back, gate_pair, pair2, edge_sel, edge_selt,
    ) = take(37)
    send_sem, recv_sem = take(2)

    def drow(m):
        return m * 8

    size_x, size_y = grid
    ix, iy = lax.axis_index("gx"), lax.axis_index("gy")

    along_x = {0: ix, 1: lax.rem(ix + 1, size_x), -1: lax.rem(ix + (size_x - 1), size_x)}
    along_y = {0: iy, 1: lax.rem(iy + 1, size_y), -1: lax.rem(iy + (size_y - 1), size_y)}

    def device(step, sign):
        return along_x[sign * step[0]], along_y[sign * step[1]]

    still = lax.div(ix, size_x)

    def lat_rows(first):
        return lat[pl.ds(pl.multiple_of(still * 8, 8) + first, 128)]

    barrier = pltpu.get_barrier_semaphore()
    for step in STEPS[::-1]:
        pl.semaphore_signal(
            barrier, inc=1, device_id=device(step, 1), device_id_type=pl.DeviceIdType.MESH
        )
    for i in FETCH_FIRST:
        fetches[i].start()
    for i in range(20):
        if i not in FETCH_FIRST:
            fetches[i].start()

    def copy(phase, k, source, target, sign, slot=None):
        slot = k if slot is None else slot
        return pltpu.make_async_remote_copy(
            src_ref=source,
            dst_ref=target,
            send_sem=send_sem.at[phase, slot],
            recv_sem=recv_sem.at[phase, slot],
            device_id=device(STEPS[k], sign),
            device_id_type=pl.DeviceIdType.MESH,
        )

    lane = iota((8, 128), 1)

    def pack(plan, k, table, target):
        groups, rows = plan[k]
        at = lane[:1]
        total = None
        for g in range(groups):
            piece = rolled(table[g * rows : (g + 1) * rows], LANES[k] * g - FIRST_LANE[k])
            total = piece if g == 0 else jnp.where(at >= LANES[k] * g, piece, total)
        target[...] = total

    def unpack_x(plan, ins):
        at = lane[:1]
        low, high = ins[0][...], ins[1][...]
        top = jnp.where(at < 64, low, rolled(high, 64))
        bottom = jnp.where(at < 64, rolled(low, 64), high)
        return jnp.concatenate([top, bottom], axis=0)

    def unpack_s(plan, ins):
        at = lane[:1]
        step = plan[4][1]
        pieces = []
        for b in range(plan[4][0]):
            value = None
            for k in range(2, 8):
                rows = plan[k][1]
                g, first = (b * step) // rows, (b * step) % rows
                piece = rolled(ins[k][first : first + step], FIRST_LANE[k] - LANES[k] * g)
                value = piece if k == 2 else jnp.where(at >= FIRST_LANE[k], piece, value)
            pieces.append(value)
        return jnp.concatenate(pieces, axis=0)

    for i in FETCH_FIRST:
        fetches[i].wait()

    def x_copies(phase, source, target, sign, chunk):
        rows = pl.ds(96 * chunk, 96)
        return [
            copy(phase, k, source[k].at[rows], target[k].at[rows], sign, k if chunk == 0 else 6 + k + 2 * chunk)
            for k in range(2)
        ]

    def pack_x(table, target, chunk):
        at = lane[:1]
        top, bottom = table[0:96], table[96:192]
        rows = slice(96 * chunk, 96 * chunk + 96)
        target[0][rows] = jnp.where(at < 64, top, rolled(bottom, 64))
        target[1][rows] = jnp.where(at < 64, rolled(top, 64), bottom)

    def unpack_x_chunk(ins, chunk):
        at = lane[:1]
        rows = slice(96 * chunk, 96 * chunk + 96)
        low, high = ins[0][rows], ins[1][rows]
        top = jnp.where(at < 64, low, rolled(high, 64))
        bottom = jnp.where(at < 64, rolled(low, 64), high)
        return jnp.concatenate([top, bottom], axis=0)

    third_rows = [slice(192 * c, 192 * c + 192) for c in range(3)]

    across, along, corner = across_ref[0, 0], along_ref[0, 0], corner_ref[0, 0]
    list_x = jnp.concatenate([across[1:2], across[0:1]], axis=1)
    list_s = jnp.concatenate(
        [along[1:2], along[0:1], corner[3:4], corner[2:3], corner[1:2], corner[0:1],
         jnp.full((1, 80), -1, jnp.int32)],
        axis=1,
    )
    lists = jnp.concatenate([list_x, list_s], axis=1)
    chosen = hot(iota((128, 256), 0) == lists)
    sel[0:128] = chosen
    sel[128:256] = chosen

    sub8 = iota((8, 128), 0)
    features = feat_ref[0, 0]
    pos_own = jnp.where(
        sub8 == 0, pos_ref[0, 0],
        jnp.where(sub8 == 1, pos_ref[1, 0], jnp.where(sub8 == 2, pos_ref[2, 0], 0.0)),
    )
    pos_high = pos_own.astype(bf16).astype(f32)
    pos_mid = (pos_own - pos_high).astype(bf16).astype(f32)
    pos_low = pos_own - pos_high - pos_mid
    own_raw = stacked(features)
    projected = dense(weight_form(jnp.transpose(pair_ref[1])), own_raw)
    raw = side_by_side(jnp.concatenate([projected, pos_own, pos_low], axis=0))
    sent = mm(raw, sel[...])
    sent = jnp.concatenate([sent[:128], sent[128:136] + sent[136:144], sent[136:144]], axis=0)
    for k in range(8):
        pack(PACK_ONE, k, sent[:, 0:128] if k < 2 else sent[:, 128:256], out1[k])

    pl.semaphore_wait(barrier, 8)
    first_copies = [copy(0, k, out1[k], in1[k], 1) for k in FARTHEST_FIRST]
    for one in first_copies:
        one.start()

    for i in (2, 3):
        fetches[i].wait()
    centre_row, neigh_row = centre_ref[0], neigh_ref[0]
    hot_c = hot(iota((128, EDGES), 0) == centre_row)
    hot_n = [hot(iota((128, EDGES), 0) + 128 * t == neigh_row) for t in range(3)]
    for t, value in enumerate([hot_c] + hot_n):
        hcn[256 * t : 256 * t + 128] = value
        hcn[256 * t + 128 : 256 * t + 256] = value
    centre_col = jnp.transpose(jnp.broadcast_to(centre_row.astype(f32), (128, EDGES)))
    neigh_col = jnp.transpose(jnp.broadcast_to(neigh_row.astype(f32), (128, EDGES)))
    lane_f = iota((1, 128), 1).astype(f32)
    hot_ct = hot(centre_col == lane_f)
    hot_nt = [hot(neigh_col == lane_f + 128.0 * t) for t in range(3)]
    for t, value in enumerate([hot_ct] + hot_nt):
        hcnt[0:EDGES, 128 * t : 128 * t + 128] = value
        hcnt[EDGES : 2 * EDGES, 128 * t : 128 * t + 128] = value
    selt_f = jnp.transpose(chosen.astype(f32)).astype(bf16)
    for t in range(2):
        selt[256 * t : 256 * t + 128] = selt_f[128 * t : 128 * t + 128]
        selt[256 * t + 128 : 256 * t + 256] = selt_f[128 * t : 128 * t + 128]

    picked = mm(hot_ct, chosen).astype(bf16)
    edge_sel[0:EDGES] = picked
    edge_sel[EDGES : 2 * EDGES] = picked
    returned_hot = mm(selt_f, hot_c).astype(bf16)
    for t in range(2):
        edge_selt[256 * t : 256 * t + 128] = returned_hot[128 * t : 128 * t + 128]
        edge_selt[256 * t + 128 : 256 * t + 256] = returned_hot[128 * t : 128 * t + 128]

    def forward_form(weight):
        return weight_form(jnp.transpose(weight))

    def pair_form(first):
        both = jnp.transpose(first)
        high, low = split(both)
        low = jnp.where(iota((1, 128), 1) < 64, low.astype(f32), 0.0).astype(bf16)
        return jnp.concatenate([high, low], axis=0)

    for i in (7, *range(9, 20)):
        fetches[i].wait()
    table1[:, 0:256] = side_by_side(dense(forward_form(pair_ref[0]), own_raw))
    table1[:, 256:512] = side_by_side(projected)
    self_rows = jnp.broadcast_to(self_ref[...].reshape(1, LAT), (16, LAT))
    self_row = dense(weight_form(self_rows), own_raw)[0:1]
    zeros64 = jnp.zeros((64, LAT), f32)
    first_t = jnp.concatenate([tensor_ref[...], gate1_ref[...]], axis=0)
    first_form[...] = weight_form(first_t)
    first_back[...] = forward_form(first_t)
    gate2_t = gate2_ref[...]
    gate2_form[...] = weight_form(gate2_t)
    gate2_back[...] = forward_form(jnp.concatenate([gate2_t, zeros64], axis=0))
    for d in range(3):
        weight = mix_ref[d]
        turned = jnp.transpose(weight)
        mix_form[d] = pair_form(jnp.concatenate([weight, weight], axis=0))
        mix_back[d] = pair_form(jnp.concatenate([turned, turned], axis=0))
    latent1_form[...] = forward_form(jnp.concatenate([latent1_ref[...], zeros64], axis=0))
    latent1_back[...] = weight_form(latent1_ref[...])
    latent2_form[...] = forward_form(jnp.concatenate([latent2_ref[...], zeros64], axis=0))
    latent2_back[...] = weight_form(latent2_ref[...])
    readout_form[...] = forward_form(readout_ref[...])
    readout_back[...] = weight_form(readout_ref[...])
    vector_col[...] = jnp.transpose(jnp.broadcast_to(vector_ref[...].reshape(1, LAT), (128, LAT)))
    radial_full = jnp.concatenate([radial_ref[...], jnp.zeros((120, LAT), f32)], axis=0)
    radial_form[...] = forward_form(radial_full)
    radial_back[...] = weight_form(radial_full[:16])

    lat[768:896] = mm(table1[:, 0:512], hcn[0:512])

    for one in first_copies[4:6]:
        one.wait()
    table_x = unpack_x(PACK_ONE, in1)
    lat[768:896] = lat_rows(768) + mm(side_by_side(table_x[:128]), hcn[512:768])
    for one in first_copies[:4] + first_copies[6:]:
        one.wait()
    table_s = unpack_s(PACK_ONE, in1)
    table1[:, 512:768] = side_by_side(table_s[:128])

    def offsets(rows):
        total = jnp.zeros((8, 128), f32)
        for k in rows:
            dx, dy = STEPS[k]
            inside = (lane >= FIRST_LANE[k]) & (lane < FIRST_LANE[k] + LANES[k])
            total = jnp.where(inside & (sub8 == 0), -1.0 * dx, total)
            total = jnp.where(inside & (sub8 == 1), -1.0 * dy, total)
        return total

    positions = jnp.concatenate(
        [pos_own, table_x[128:136] + offsets((0, 1)), table_s[128:136] + offsets(range(2, 8))], axis=1
    )
    p_high = positions.astype(bf16).astype(f32)
    p_mid = (positions - p_high).astype(bf16).astype(f32)
    p_low = positions - p_high - p_mid
    parts = jnp.concatenate([p_high, p_mid, p_low, jnp.zeros_like(p_low)], axis=0).astype(bf16)
    moved = mm(parts[:, 0:128], hcn[256:384] - hcn[0:128])
    moved += mm(parts[:, 128:256], hcn[512:640]) + mm(parts[:, 256:384], hcn[768:896])
    moved = moved[0:8] + moved[8:16] + moved[16:24]

    length = jnp.sqrt(jnp.sum(moved * moved, axis=0, keepdims=True) + 0.25)
    inverse = 1.0 / length
    unit = moved * inverse
    ux, uy, uz = unit[0:1], unit[1:2], unit[2:3]
    live = (iota((1, EDGES), 1) < edge_count_ref[...]).astype(f32)
    falloff = 1.0 / (1.0 + 0.25 * length * length)
    envelope = live * falloff
    square = ux * ux + uy * uy + uz * uz
    shapes = [
        jnp.ones_like(ux), ux, uy, uz, ROOT3 * ux * uy, ROOT3 * uy * uz,
        0.5 * (3.0 * uz * uz - square), ROOT3 * ux * uz, 0.5 * ROOT3 * (ux * ux - uy * uy),
    ]
    for m in range(9):
        geo[drow(m) : drow(m) + 8] = jnp.broadcast_to(shapes[m], (8, EDGES))
    geo[72:80] = jnp.broadcast_to(envelope, (8, EDGES))

    mid_points = 0.5 + WIDTH * iota((BASIS, EDGES), 0).astype(f32)
    scaled = (length - mid_points) / WIDTH
    basis = jnp.exp(-(scaled * scaled))
    basis_full = jnp.concatenate([basis, jnp.zeros((120, EDGES), f32)], axis=0)
    before0 = dense(radial_form[...], stacked(basis_full)) + lat_rows(768)
    before0 = before0 + mm(table1[:, 512:768], hcn[768:1024])
    latent0, slope0 = sigmoid_parts(before0)
    lat[0:128] = slope0
    lat[128:256] = latent0
    high0, low0 = split(latent0)
    pile[0:128] = high0
    pile[384:512] = low0
    gains = dense(first_form[...], jnp.concatenate([high0, low0], axis=0))
    grads[0:128] = gains

    def lanes_at(t):
        return pl.ds(pl.multiple_of(t * 128, 128), 128)

    def shape_at(m, at):
        return geo[m * 8 : m * 8 + 1, at]

    def write_wide(row, t, value):
        high, low = split(value)
        wide[row : row + 16, lanes_at(t)] = high
        wide[row : row + 16, lanes_at(t + 4)] = low

    def spread(source, row0, members):
        def tile(t, carry):
            at = lanes_at(t)
            weight = 0.5 * geo[72:73, at]
            for c in range(4):
                gate = source[row0 + 16 * c : row0 + 16 * c + 16, at] * weight
                for m in members:
                    value = gate if m == 0 else gate * shape_at(m, at)
                    write_wide(64 * m + 16 * c, t, value)
            return carry

        lax.fori_loop(0, 4, tile, 0)

    second_x, sent = [], []
    second_copies = [copy(1, k, out2[k], in2[k], 1) for k in range(2, 8)]
    for c in range(3):
        spread(grads, 64, MEMBERS[c])
        sent.append(mm(wide[third_rows[c]], edge_sel[...]))
        if c == 2:
            rest = jnp.concatenate([part[:, 128:256] for part in sent], axis=0)
            for k in (4, 5, 6, 7, 2, 3):
                pack(PACK_TWO, k, rest, out2[k])
                second_copies[k - 2].start()
        pack_x(sent[c][:, 0:128], out2, c)
        second_x.append(x_copies(1, out2, in2, 1, c))
        for one in second_x[c]:
            one.start()

    table2[:, 256:512] = side_by_side(mm(wide[...], hcnt[:, 0:128]))
    g1[...] = mm(table2[:, 256:512], hcn[0:256])

    def couple(t, carry):
        at = lanes_at(t)
        y = [None] + [shape_at(m, at) for m in range(1, 9)]
        for c in range(4):
            gain = grads[16 * c : 16 * c + 16, at]
            g = [g1[64 * m + 16 * c : 64 * m + 16 * c + 16, at] for m in range(9)]
            inner = [g[0] + g[0]] + [y[m] * g[0] + g[m] for m in range(1, 9)]
            inner[1] = inner[1] + (y[2] * g[3] - y[3] * g[2])
            inner[2] = inner[2] + (y[3] * g[1] - y[1] * g[3])
            inner[3] = inner[3] + (y[1] * g[2] - y[2] * g[1])
            for m in range(9):
                high, low = split(gain * inner[m])
                mixed[m, 16 * c : 16 * c + 16, at] = high
                mixed[m, 64 + 16 * c : 80 + 16 * c, at] = low
            sums = [
                g[0],
                y[1] * g[1] + y[2] * g[2] + y[3] * g[3],
                y[4] * g[4] + y[5] * g[5] + y[6] * g[6] + y[7] * g[7] + y[8] * g[8],
            ]
            for d in range(3):
                high, low = split(gain * sums[d])
                row = 128 + 64 * d + 16 * c
                pile[row : row + 16, at] = high
                pile[384 + row : 400 + row, at] = low
        return carry

    lax.fori_loop(0, 4, couple, 0)
    nothing = jnp.zeros((64, EDGES), bf16)
    pile[320:384] = nothing
    pile[704:768] = nothing
    act1, slope1 = sigmoid_parts(dense(latent1_form[...], pile[...]))
    lat[256:384] = slope1
    latent1 = lat_rows(128) + act1
    lat[384:512] = latent1
    high1, low1 = split(latent1)
    early = jnp.concatenate([latent2_form[:, 0:128], latent2_form[:, 384:512]], axis=1)
    lat[896:1024] = dense(early, jnp.concatenate([high1, low1], axis=0))
    grads[128:192] = dense(gate2_form[...], jnp.concatenate([high1, low1], axis=0))
    spread(grads, 128, range(9))
    table2[:, 0:256] = side_by_side(mm(wide[...], hcnt[:, 0:128]))
    joint[...] = mm(table2[...], hcn[0:512])
    for m in range(9):
        t1[64 * m : 64 * m + 64] = dense(mix_form[DEGREE[m]], mixed[m])

    for c in range(2):
        for one in second_x[c]:
            one.wait()
        joint[third_rows[c]] += mm(side_by_side(unpack_x_chunk(in2, c)), hcn[512:768])
    for one in second_copies:
        one.wait()
    joint[...] += mm(side_by_side(unpack_s(PACK_TWO, in2)), hcn[768:1024])

    def contract(degrees):
        def tile(t, carry):
            at = lanes_at(t)
            for c in range(4):
                for d in degrees:
                    total = None
                    for m in range(9):
                        if DEGREE[m] == d:
                            row = 64 * m + 16 * c
                            term = t1[row : row + 16, at] * joint[row : row + 16, at]
                            total = term if total is None else total + term
                    high, low = split(total)
                    row = 128 + 64 * d + 16 * c
                    pile[row : row + 16, at] = high
                    pile[384 + row : 400 + row, at] = low
            return carry

        lax.fori_loop(0, 4, tile, 0)

    contract((0, 1))
    part = jnp.concatenate([latent2_form[:, 128:256], latent2_form[:, 512:640]], axis=1)
    part_pile = jnp.concatenate([pile[128:256], pile[512:640]], axis=0)
    lat[896:1024] = lat_rows(896) + dense(part, part_pile)
    for one in second_x[2]:
        one.wait()
    joint[384:576] += mm(side_by_side(unpack_x_chunk(in2, 2)), hcn[512:768])
    contract((2,))
    late = jnp.concatenate([latent2_form[:, 256:384], latent2_form[:, 640:768]], axis=1)
    late_pile = jnp.concatenate([pile[256:384], pile[640:768]], axis=0)
    act2, slope2 = sigmoid_parts(lat_rows(896) + dense(late, late_pile))
    latent2 = lat_rows(384) + act2
    hidden, slope_h = sigmoid_parts(dense(readout_form[...], stacked(latent2)))
    vector_wide = jnp.concatenate([vector_col[...]] * 4, axis=1)
    energy_raw = jnp.sum(vector_wide * hidden, axis=0, keepdims=True)
    edge_energy = envelope * energy_raw

    d_hidden = vector_wide * envelope * slope_h
    d_latent2 = dense(readout_back[...], stacked(d_hidden))
    d_before2 = stacked(d_latent2 * slope2)
    grads[192:384] = mm(latent2_back[128:320], d_before2) + mm(latent2_back[448:640], d_before2)
    lat[512:640] = d_latent2
    pair2[...] = d_before2

    def joint_back(members):
        def tile(t, carry):
            at = lanes_at(t)
            for c in range(4):
                d_sum = [grads[192 + 64 * d + 16 * c : 208 + 64 * d + 16 * c, at] for d in range(3)]
                for m in members:
                    row = 64 * m + 16 * c
                    write_wide(row, t, t1[row : row + 16, at] * d_sum[DEGREE[m]])
            return carry

        lax.fori_loop(0, 4, tile, 0)

    third_x, sent = [], []
    third_copies = [copy(2, k, out3[k], in3[k], -1) for k in range(2, 8)]
    for c in range(3):
        joint_back(MEMBERS[c])
        sent.append(mm(wide[third_rows[c]], hcnt[:, 256:512]))
        if c == 2:
            rest = jnp.concatenate([part[:, 128:256] for part in sent], axis=0)
            for k in (4, 5, 6, 7, 2, 3):
                pack(PACK_TWO, k, rest, out3[k])
                third_copies[k - 2].start()
        pack_x(sent[c][:, 0:128], out3, c)
        third_x.append(x_copies(2, out3, in3, -1, c))
        for one in third_x[c]:
            one.start()

    both = mm(latent2_back[0:128], pair2[...]) + mm(latent2_back[320:448], pair2[...])
    lat[512:640] = lat_rows(512) + both
    back = mm(wide[...], hcnt[:, 0:256])
    env_own[...] = back[:, 128:256]
    big[...] = mm(side_by_side(back[:, 0:128]), hcn[0:256])

    def mix_grads(t, carry):
        at = lanes_at(t)
        for c in range(4):
            d_sum = [grads[192 + 64 * d + 16 * c : 208 + 64 * d + 16 * c, at] for d in range(3)]
            for m in range(9):
                row = 64 * m + 16 * c
                high, low = split(joint[row : row + 16, at] * d_sum[DEGREE[m]])
                mixed[m, 16 * c : 16 * c + 16, at] = high
                mixed[m, 64 + 16 * c : 80 + 16 * c, at] = low
        return carry

    lax.fori_loop(0, 4, mix_grads, 0)
    for m in range(9):
        joint[64 * m : 64 * m + 64] = dense(mix_back[DEGREE[m]], mixed[m])

    def halves(value):
        return value[0:8] + value[8:16]

    def spread_back(source, row0, target0, members, fresh, first, last):
        def tile(t, carry):
            at = lanes_at(t)
            half = 0.5 * geo[72:73, at]
            d_shape = [None] * 9
            d_env = None
            for c in range(4):
                gate = source[row0 + 16 * c : row0 + 16 * c + 16, at]
                weight = gate * half
                total = None if first else grads[target0 + 16 * c : target0 + 16 * c + 16, at]
                for m in members:
                    row = 64 * m + 16 * c
                    value = big[row : row + 16, at]
                    if m:
                        term = halves(value * weight)
                        d_shape[m] = term if c == 0 else d_shape[m] + term
                        value = value * shape_at(m, at)
                    total = value if total is None else total + value
                if last:
                    term = halves(total * gate)
                    d_env = term if c == 0 else d_env + term
                    total = total * half
                grads[target0 + 16 * c : target0 + 16 * c + 16, at] = total
            for m in members:
                if m and fresh:
                    acc[drow(m) : drow(m) + 8, at] = d_shape[m]
                elif m:
                    acc[drow(m) : drow(m) + 8, at] += d_shape[m]
            if last and fresh:
                acc[0:8, at] = 0.5 * d_env
            elif last:
                acc[0:8, at] += 0.5 * d_env
            return carry

        lax.fori_loop(0, 4, tile, 0)

    spread_back(grads, 128, 384, range(9), True, True, True)
    gate_high, gate_low = split(grads[384:448])
    gate_pair[0:64] = gate_high
    gate_pair[64:128] = nothing
    gate_pair[128:192] = gate_low
    gate_pair[192:256] = nothing
    d_latent1 = lat_rows(512) + dense(gate2_back[...], gate_pair[...])
    d_pile = dense(latent1_back[...], stacked(d_latent1 * lat_rows(256)))
    lat[640:768] = d_latent1 + d_pile[0:128]
    grads[192:384] = d_pile[128:320]

    def couple_back(t, carry):
        at = lanes_at(t)
        y = [None] + [shape_at(m, at) for m in range(1, 9)]
        d_shape = [None] * 9
        for c in range(4):
            gain = grads[16 * c : 16 * c + 16, at]
            g = [g1[64 * m + 16 * c : 64 * m + 16 * c + 16, at] for m in range(9)]
            u = [joint[64 * m + 16 * c : 64 * m + 16 * c + 16, at] for m in range(9)]
            s = [grads[192 + 64 * d + 16 * c : 208 + 64 * d + 16 * c, at] for d in range(3)]
            inner = [g[0] + g[0]] + [y[m] * g[0] + g[m] for m in range(1, 9)]
            inner[1] = inner[1] + (y[2] * g[3] - y[3] * g[2])
            inner[2] = inner[2] + (y[3] * g[1] - y[1] * g[3])
            inner[3] = inner[3] + (y[1] * g[2] - y[2] * g[1])
            d_gain = s[0] * g[0]
            for m in range(9):
                d_gain = d_gain + u[m] * inner[m]
            d_gain = d_gain + s[1] * (y[1] * g[1] + y[2] * g[2] + y[3] * g[3])
            d_gain = d_gain + s[2] * (
                y[4] * g[4] + y[5] * g[5] + y[6] * g[6] + y[7] * g[7] + y[8] * g[8]
            )
            grads[448 + 16 * c : 464 + 16 * c, at] = d_gain
            k = [gain * value for value in u]
            q = [gain * value for value in s]
            d_g = [k[0] + k[0] + q[0]] + [k[m] + q[DEGREE[m]] * y[m] for m in range(1, 9)]
            for m in range(1, 9):
                d_g[0] = d_g[0] + k[m] * y[m]
            d_g[1] = d_g[1] + (k[2] * y[3] - k[3] * y[2])
            d_g[2] = d_g[2] + (k[3] * y[1] - k[1] * y[3])
            d_g[3] = d_g[3] + (k[1] * y[2] - k[2] * y[1])
            d_y = [None] + [k[m] * g[0] + q[DEGREE[m]] * g[m] for m in range(1, 9)]
            d_y[1] = d_y[1] + (k[3] * g[2] - k[2] * g[3])
            d_y[2] = d_y[2] + (k[1] * g[3] - k[3] * g[1])
            d_y[3] = d_y[3] + (k[2] * g[1] - k[1] * g[2])
            for m in range(1, 9):
                term = halves(d_y[m])
                d_shape[m] = term if c == 0 else d_shape[m] + term
            for m in range(9):
                write_wide(64 * m + 16 * c, t, d_g[m])
        for m in range(1, 9):
            acc[drow(m) : drow(m) + 8, at] += d_shape[m]
        return carry

    lax.fori_loop(0, 4, couple_back, 0)
    env_own[...] += mm(wide[...], hcnt[:, 0:128])

    big[...] = mm(side_by_side(env_own[...]), hcn[0:256])
    for c in range(2):
        for one in third_x[c]:
            one.wait()
        big[third_rows[c]] += mm(side_by_side(unpack_x_chunk(in3, c)), edge_selt[0:256])
    for one in third_copies:
        one.wait()
    big[...] += mm(side_by_side(unpack_s(PACK_TWO, in3)), edge_selt[256:512])
    spread_back(grads, 64, 512, range(6), False, True, False)
    for one in third_x[2]:
        one.wait()
    big[384:576] += mm(side_by_side(unpack_x_chunk(in3, 2)), edge_selt[0:256])
    spread_back(grads, 64, 512, range(6, 9), False, False, True)
    d_latent0 = lat_rows(640) + dense(first_back[...], stacked(grads[448:576]))
    d_basis = dense(radial_back[...], stacked(d_latent0 * lat_rows(0)))[:8]
    d_length = jnp.sum(d_basis * basis * scaled, axis=0, keepdims=True) * (-2.0 / WIDTH)
    d_env = jnp.sum(acc[0:8], axis=0, keepdims=True) + energy_raw
    d_length = d_length - 0.5 * length * envelope * falloff * d_env
    d_y = [None] + [jnp.sum(acc[drow(m) : drow(m) + 8], axis=0, keepdims=True) for m in range(1, 9)]
    d_ux = d_y[1] + ROOT3 * (uy * d_y[4] + uz * d_y[7] + ux * d_y[8]) - ux * d_y[6]
    d_uy = d_y[2] + ROOT3 * (ux * d_y[4] + uz * d_y[5] - uy * d_y[8]) - uy * d_y[6]
    d_uz = d_y[3] + ROOT3 * (uy * d_y[5] + ux * d_y[7]) + 2.0 * (uz * d_y[6])
    d_length = d_length - (d_ux * ux + d_uy * uy + d_uz * uz) * inverse
    sub_e = iota((8, EDGES), 0)
    d_unit = jnp.where(sub_e == 0, d_ux, jnp.where(sub_e == 1, d_uy, jnp.where(sub_e == 2, d_uz, 0.0)))
    d_moved = d_unit * inverse + d_length * unit

    def folded(value):
        high = value.astype(bf16).astype(f32)
        return jnp.concatenate([high, value - high], axis=0).astype(bf16)

    d_parts = folded(d_moved)
    d_table = halves(mm(d_parts, hcnt[0:EDGES, 128:512]))
    d_centre = halves(mm(d_parts, hcnt[0:EDGES, 0:128]))
    out4[0][...] = d_table[:, 128:256]
    out4[1][...] = d_table[:, 256:384]
    last_copies = [copy(3, k, out4[0] if k < 2 else out4[1], in4[k], -1) for k in FARTHEST_FIRST]
    for one in last_copies:
        one.start()
    d_own = d_table[:, 0:128] - d_centre

    per_atom = halves(mm(folded(jnp.broadcast_to(edge_energy, (8, EDGES))), hcnt[0:EDGES, 0:128]))[0:1]
    alive = (iota((1, ATOMS), 1) < atom_count_ref[...]).astype(f32)
    out_ref[3, 0] = -(alive * (per_atom + self_row))

    for one in last_copies:
        one.wait()
    grad_x = jnp.where(lane < 64, in4[0][...], in4[1][...])
    grad_s = in4[2][...]
    for k in range(3, 8):
        grad_s = jnp.where(lane >= FIRST_LANE[k], in4[k][...], grad_s)
    returned = mm(folded(grad_x), selt[0:128]) + mm(folded(grad_s), selt[256:384])
    total = d_own + halves(returned)
    for axis in range(3):
        out_ref[axis, 0] = total[axis : axis + 1]


def per_device(grid, *args):
    args = list(args)
    for i in (11, 12, 15):
        args[i] = args[i].T
    sources = args[:2] + args[4:] + args[2:4]
    vmem = pl.BlockSpec(memory_space=pltpu.VMEM)
    specs = [pl.BlockSpec(memory_space=pltpu.HBM)] * 20
    packs = [
        [pltpu.VMEM((plan[k][1], 128), f32) for k in range(8)] for plan in (PACK_ONE, PACK_TWO)
    ]
    small = [pltpu.VMEM((8, 128), f32)]
    scratch = [pltpu.VMEM(source.shape, source.dtype) for source in sources]
    scratch += [pltpu.SemaphoreType.DMA((20,))]
    scratch += packs[0] * 2 + packs[1] * 4 + small * 8 + small * 2
    scratch += [
        pltpu.VMEM((1024, EDGES), bf16),
        pltpu.VMEM((2 * EDGES, 512), bf16),
        pltpu.VMEM((256, 256), bf16),
        pltpu.VMEM((512, 128), bf16),
        pltpu.VMEM((128, 768), bf16),
        pltpu.VMEM((576, 512), bf16),
        pltpu.VMEM((80, EDGES), f32),
        pltpu.VMEM((1024, EDGES), f32),
        pltpu.VMEM((576, EDGES), f32),
        pltpu.VMEM((576, EDGES), f32),
        pltpu.VMEM((576, EDGES), f32),
        pltpu.VMEM((576, EDGES), f32),
        pltpu.VMEM((576, EDGES), f32),
        pltpu.VMEM((576, 2 * EDGES), bf16),
        pltpu.VMEM((9, 128, EDGES), bf16),
        pltpu.VMEM((768, EDGES), bf16),
        pltpu.VMEM((72, EDGES), f32),
        pltpu.VMEM((576, 128), f32),
        *(
            pltpu.VMEM(shape, bf16)
            for shape in (
                (256, 256), (256, 256), (128, 256), (256, 256), (3, 128, 128),
                (3, 128, 128), (256, 768), (640, 256), (256, 768), (640, 256), (256, 256), (256, 256),
            )
        ),
        pltpu.VMEM((128, 128), f32),
        pltpu.VMEM((256, 256), bf16),
        pltpu.VMEM((32, 256), bf16),
        pltpu.VMEM((256, EDGES), bf16),
        pltpu.VMEM((256, EDGES), bf16),
        pltpu.VMEM((2 * EDGES, 256), bf16),
        pltpu.VMEM((512, EDGES), bf16),
        pltpu.SemaphoreType.DMA((4, 12)),
        pltpu.SemaphoreType.DMA((4, 12)),
    ]
    result = pl.pallas_call(
        functools.partial(body, grid),
        out_shape=jax.ShapeDtypeStruct((4, 1, 1, ATOMS), f32),
        in_specs=specs,
        out_specs=vmem,
        scratch_shapes=scratch,
        compiler_params=pltpu.CompilerParams(
            collective_id=0, has_side_effects=True, vmem_limit_bytes=64 * 1024 * 1024
        ),
    )(*sources)
    result = -result
    return result[:3], result[3]


def solution(mesh):
    grid = (mesh.shape["gx"], mesh.shape["gy"])
    edge = P("gx", "gy", None)
    lists = P("gx", "gy", None, None)
    return jax.shard_map(
        functools.partial(per_device, grid),
        mesh=mesh,
        in_specs=(P(None, "gx", "gy", None), lists, P("gx", "gy"), P("gx", "gy"), edge, edge)
        + (lists,) * 3
        + (P(),) * 11,
        out_specs=(P(None, "gx", "gy", None), edge),
        check_vma=False,
    )
```
